32 devices in a mesh: inp: 4 (over z), tgt: 4 (over x, core), mdl: 2 (over y).
Axes of the slice: x: 2, y: 2, z: 4, core: 2. Of those that a mesh axis runs over, the one named last changes fastest.
Arguments:
- encoder: bfloat16 [2048, 4096], P('inp'), may hold values from -8 to 8
- key_weight: bfloat16 [2, 4096, 2, 4, 256], P(None, None, 'mdl', 'tgt'), may hold values from -1 to 1
- value_weight: bfloat16 [2, 4096, 2, 4, 256], P(None, None, 'mdl', 'tgt'), may hold values from -0.09375 to 0.09375
- queries: bfloat16 [2, 2048, 8, 256], P(None, 'tgt', 'mdl'), may hold values from -8 to 8
- grad_out: bfloat16 [2, 2048, 8, 256], P(None, 'tgt', 'mdl'), may hold values from -6 to 6
Outputs:
- grad_query: bfloat16 [2, 2048, 8, 256], P(None, 'tgt', 'mdl')
- grad_encoder: bfloat16 [2048, 4096], P('inp', ('tgt', 'mdl'))
The draws below stay inside these ranges and needn't reach their ends.
All inputs are finite; a program needn't handle non-finite values.
Results may differ from the reference program's by a relative error of at most 0.019.
The reference program's roundings to bfloat16 on the way count: a program that leaves them out, or rounds other values in their place, can miss the bound.
Values may be sent and summed in bfloat16 or wider, within the bound.
No kernel may reach another device: no remote copies, remote signals or barrier semaphores. Data moves between devices by JAX's collectives and lax.ppermute only.
A program may use at most 128 MiB of HBM per device.

```python
import math
import jax
import jax.numpy as jnp
from jax import lax

D = 4096
HEADS = 8
HS = 256
LAYERS = 2
ENC = 2048
DEC = 2048
HPG = 4
N_MDL = 2


def encoder_row(source, row_index):
    row_key = jax.random.fold_in(jax.random.fold_in(source, 101), row_index)
    row_values = jnp.clip(jax.random.normal(row_key, (D,), jnp.float32), -6.0, 6.0)
    rising = 0.8 + 0.5 * row_index.astype(jnp.float32) / ENC
    return row_values * rising


def key_weight_flat(source):
    weight_key = jax.random.fold_in(source, 102)
    raw_values = jax.random.normal(weight_key, (LAYERS, D, HEADS, HS), jnp.float32)
    return jnp.clip(raw_values, -4.0, 4.0) / math.sqrt(D)


def draw_encoder(key, part):
    positions = jnp.arange(ENC, dtype=jnp.int32)
    values = jax.vmap(lambda row_index: encoder_row(key, row_index))(positions)
    return values.astype(jnp.bfloat16)


def draw_key_weight(key, part):
    values = key_weight_flat(key).reshape(LAYERS, D, HEADS // HPG, HPG, HS)
    return values.astype(jnp.bfloat16)


def draw_queries(key, part):
    key = jax.random.fold_in(key, 3)
    values = jnp.clip(jax.random.normal(key, (LAYERS, DEC, HEADS, HS), jnp.float32), -6.0, 6.0) * 0.12
    return values.astype(jnp.bfloat16)


def block_levels(rng, extent, pieces, least, top_value):
    def one(position, blocks):
        draws = jax.random.uniform(jax.random.fold_in(jax.random.fold_in(rng, 6), position), (blocks,), jnp.float32, least / len(pieces), top_value / len(pieces))
        return jnp.repeat(jnp.exp(draws), extent[position] // blocks).reshape((-1,) + (1,) * (len(extent) - position - 1))

    loudness = one(*pieces[0])
    for cut in pieces[1:]:
        loudness = loudness * one(*cut)
    return loudness


def bell_draw(key, dims, deviation, limit, cuts=(), kind=jnp.bfloat16):
    values = deviation * jax.random.normal(key, dims, jnp.float32)
    if cuts:
        values = values * block_levels(key, dims, cuts, -0.22, 0.18)
    return jnp.clip(values, -limit, limit).astype(kind)


def setup_inputs(seed: int = 0) -> dict:
    streams_of = jax.random.split(jax.random.key(seed), 6)
    encoder = draw_encoder(jax.random.fold_in(streams_of[5], 71), 0)
    key_weight = draw_key_weight(jax.random.fold_in(streams_of[5], 71), 0)
    value_weight = bell_draw(streams_of[2], (LAYERS, D, N_MDL, HPG, HS), D ** -0.5, 0.09375, ((2, 2), (3, 4)))
    queries = draw_queries(jax.random.fold_in(streams_of[5], 71), 0)
    grad_out = bell_draw(streams_of[4], (LAYERS, DEC, HEADS, HS), 1.0, 6.0, ((1, 4), (2, 2)))
    return {"encoder": encoder, "key_weight": key_weight, "value_weight": value_weight, "queries": queries, "grad_out": grad_out}


def head_grads(operands):
    query_head, grad_head, key_head, value_head = operands
    scores = jnp.dot(query_head, key_head.T, preferred_element_type=jnp.float32)
    shifted = jnp.exp(scores - jnp.max(scores, axis=1, keepdims=True))
    attention = shifted / jnp.sum(shifted, axis=1, keepdims=True)
    dprobs = jnp.dot(grad_head, value_head.T, preferred_element_type=jnp.float32)
    row_inner = jnp.sum(attention * dprobs, axis=1, keepdims=True)
    dscores = (attention * (dprobs - row_inner)).astype(jnp.bfloat16)
    attention_low = attention.astype(jnp.bfloat16)
    query_grad = jnp.dot(dscores, key_head, preferred_element_type=jnp.float32).astype(jnp.bfloat16)
    key_grad = jnp.dot(dscores.T, query_head, preferred_element_type=jnp.float32).astype(jnp.bfloat16)
    value_grad = jnp.dot(attention_low.T, grad_head, preferred_element_type=jnp.float32).astype(jnp.bfloat16)
    return query_grad, key_grad, value_grad


def reference(encoder, key_weight, value_weight, queries, grad_out):
    grad_layers = []
    enc_grad = jnp.zeros((ENC, D), jnp.float32)
    for layer_index in range(LAYERS):
        key_matrix = key_weight[layer_index].reshape(D, HEADS * HS)
        value_matrix = value_weight[layer_index].reshape(D, HEADS * HS)
        key_block = jnp.dot(encoder, key_matrix, preferred_element_type=jnp.float32).astype(jnp.bfloat16).reshape(ENC, HEADS, HS)
        value_block = jnp.dot(encoder, value_matrix, preferred_element_type=jnp.float32).astype(jnp.bfloat16).reshape(ENC, HEADS, HS)
        operands = (jnp.swapaxes(queries[layer_index], 0, 1), jnp.swapaxes(grad_out[layer_index], 0, 1),
                    jnp.swapaxes(key_block, 0, 1), jnp.swapaxes(value_block, 0, 1))
        query_grad, key_grad, value_grad = lax.map(head_grads, operands)
        grad_layers.append(jnp.swapaxes(query_grad, 0, 1))
        key_flat = jnp.swapaxes(key_grad, 0, 1).reshape(ENC, HEADS * HS)
        value_flat = jnp.swapaxes(value_grad, 0, 1).reshape(ENC, HEADS * HS)
        enc_grad = enc_grad + jnp.dot(key_flat, key_matrix.T, preferred_element_type=jnp.float32)
        enc_grad = enc_grad + jnp.dot(value_flat, value_matrix.T, preferred_element_type=jnp.float32)
    return jnp.stack(grad_layers), enc_grad.astype(jnp.bfloat16)
```

```python
import functools

import jax
import jax.numpy as jnp
from jax import lax
from jax.experimental import pallas as pl
from jax.experimental.pallas import tpu as pltpu
from jax.sharding import PartitionSpec as P

F32, BF16 = jnp.float32, jnp.bfloat16
VMEM_BYTES = 48 * 1024 * 1024
NT = (((1,), (1,)), ((), ()))
NN = (((1,), (0,)), ((), ()))
TN = (((0,), (0,)), ((), ()))


def dot(left, right, dims):
    return lax.dot_general(left, right, dims, preferred_element_type=F32)


def params():
    return pltpu.CompilerParams(vmem_limit_bytes=VMEM_BYTES)


def cost(flops, nbytes, exps=0):
    return pl.CostEstimate(flops=1, bytes_accessed=1, transcendentals=0)


def partners(count, mask):
    return [(index, index ^ mask) for index in range(count)]


def join_kernel(rank_ref, *refs):
    out, held = refs[-2], refs[-1]
    heads = held.shape[0]

    @pl.when(rank_ref[1] == 0)
    def _():
        for mask in range(heads):
            held[mask] = refs[mask][0]

    @pl.when(rank_ref[1] != 0)
    def _():
        for mask in range(heads):
            held[mask] = refs[heads + mask][0]

    for head in range(heads):
        out[0, :, head, :] = held[rank_ref[0] ^ head]


def join_heads(rank, pieces, layer, layers, begun):
    heads = len(pieces) // 2
    rows, size = pieces[0][0].shape[1:]

    def place(index):
        return pl.BlockSpec((1, rows, size), lambda i, rank: (index, 0, 0))

    extra = [] if begun is None else [begun]
    return pl.pallas_call(
        join_kernel,
        grid_spec=pltpu.PrefetchScalarGridSpec(
            num_scalar_prefetch=1,
            grid=(1,),
            in_specs=[place(index) for _, index in pieces] + [pl.BlockSpec(memory_space=pl.ANY)] * len(extra),
            out_specs=pl.BlockSpec((1, rows, heads, size), lambda i, rank: (layer, 0, 0, 0)),
            scratch_shapes=[pltpu.VMEM((heads, rows, size), BF16)],
        ),
        out_shape=jax.ShapeDtypeStruct((layers, rows, heads, size), BF16),
        input_output_aliases={1 + len(pieces): 0} if extra else {},
        compiler_params=params(),
        cost_estimate=cost(0, 8 * rows * heads * size),
    )(rank, *[piece for piece, _ in pieces], *extra)


def project_kernel(enc_ref, wk_ref, wv_ref, k_ref, v_ref, sums):
    step = pl.program_id(0)

    @pl.when(step == 0)
    def _():
        sums[...] = jnp.zeros_like(sums)

    sums[0] += dot(enc_ref[...], wk_ref[0], NN)
    sums[1] += dot(enc_ref[...], wv_ref[0], NN)

    @pl.when(step == pl.num_programs(0) - 1)
    def _():
        k_ref[...] = sums[0].astype(BF16)
        v_ref[...] = sums[1].astype(BF16)


def project(encoder, wk, wv, layer):
    rows, width = encoder.shape
    size = wk.shape[2]
    depth = width // 4
    weight = pl.BlockSpec((1, depth, size), lambda i: (layer, i, 0))
    result = pl.BlockSpec((rows, size), lambda i: (0, 0))
    return pl.pallas_call(
        project_kernel,
        grid=(width // depth,),
        in_specs=[pl.BlockSpec((rows, depth), lambda i: (0, i)), weight, weight],
        out_specs=[result, result],
        out_shape=[jax.ShapeDtypeStruct((rows, size), BF16)] * 2,
        scratch_shapes=[pltpu.VMEM((2, rows, size), F32)],
        compiler_params=params(),
        cost_estimate=cost(4 * rows * width * size, 2 * width * (rows + 2 * size)),
    )(encoder, wk, wv)


def columns(index, count, rows, flip_ref):
    if index < count - 2:
        return slice(index * rows, (index + 1) * rows)
    start = (count - 2 + ((index - count + 2) ^ flip_ref[0])) * rows
    return pl.ds(pl.multiple_of(start, rows), rows)


def stats_kernel(flip_ref, k_ref, v_ref, *refs):
    out, pieces = refs[-1], refs[:-1]
    count = len(pieces) // 2
    for index in range(count):
        rows = pieces[index].shape[1]
        cols = columns(index, count, rows, flip_ref)
        scores = dot(k_ref[...], pieces[index][0], NT)
        peak = jnp.max(scores, axis=0, keepdims=True)
        shifted = jnp.exp(scores - peak)
        dprobs = dot(v_ref[...], pieces[count + index][0], NT)
        out[0:1, cols] = peak
        out[1:2, cols] = jnp.sum(shifted, axis=0, keepdims=True)
        out[2:3, cols] = jnp.sum(shifted * dprobs, axis=0, keepdims=True)
        out[3:4, cols] = jnp.zeros_like(peak)


def whole(shape):
    return pl.BlockSpec(shape, lambda i: (0,) * len(shape))


def of_layer(array, layer):
    index = layer if array.shape[0] > 1 else 0
    return pl.BlockSpec((1,) + array.shape[1:], lambda i: (index, 0, 0))


def row_stats(flip, keys, values, pieces, layer):
    enc_rows, size = keys.shape
    total = pieces[0].shape[1] * len(pieces) // 2
    return pl.pallas_call(
        stats_kernel,
        grid=(1,),
        in_specs=[pl.BlockSpec(memory_space=pltpu.SMEM), whole(keys.shape), whole(values.shape)]
        + [of_layer(array, layer) for array in pieces],
        out_specs=whole((4, total)),
        out_shape=jax.ShapeDtypeStruct((4, total), F32),
        compiler_params=params(),
        cost_estimate=cost(
            4 * enc_rows * total * size, 4 * size * (enc_rows + total), enc_rows * total
        ),
    )(flip, keys, values, *pieces)


def grads_kernel(count, flip_ref, k_ref, v_ref, *refs):
    queries, cotangents, stats = refs[:count], refs[count : 2 * count], refs[2 * count : -5]
    near_ref, straight_ref, across_ref, dk_ref, dv_ref = refs[-5:]
    keys, values = k_ref[...], v_ref[...]
    grads = []
    for index in range(count):
        query, cotangent = queries[index][0], cotangents[index][0]
        cols = columns(index, count, query.shape[0], flip_ref)
        parts = [part[:, cols] for part in stats]
        peak = functools.reduce(jnp.maximum, [part[0:1] for part in parts])
        scales = [jnp.exp(part[0:1] - peak) for part in parts]
        total = sum(part[1:2] * scale for part, scale in zip(parts, scales))
        inner = sum(part[2:3] * scale for part, scale in zip(parts, scales)) / total
        attention = jnp.exp(dot(keys, query, NT) - peak) * (1.0 / total)
        dprobs = dot(values, cotangent, NT)
        dscores = (attention * (dprobs - inner)).astype(BF16)
        query_grad = dot(dscores, keys, TN).astype(BF16)
        if index < count - 2:
            near_ref[index] = query_grad
        else:
            grads.append(query_grad)
        key_part = dot(dscores, query, NN)
        value_part = dot(attention.astype(BF16), cotangent, NN)
        key_sum = key_part if index == 0 else key_sum + key_part
        value_sum = value_part if index == 0 else value_sum + value_part
    dk_ref[...] = key_sum.astype(BF16)
    dv_ref[...] = value_sum.astype(BF16)

    @pl.when(flip_ref[0] == 0)
    def _():
        straight_ref[0], across_ref[0] = grads

    @pl.when(flip_ref[0] != 0)
    def _():
        across_ref[0], straight_ref[0] = grads


def attention_grads(flip, keys, values, pieces, stats, layer):
    enc_rows, size = keys.shape
    rows = pieces[0].shape[1]
    count = len(pieces) // 2
    total = rows * count
    outs = [(count - 2, rows, size), (1, rows, size), (1, rows, size), (enc_rows, size), (enc_rows, size)]
    return pl.pallas_call(
        functools.partial(grads_kernel, count),
        grid=(1,),
        in_specs=[pl.BlockSpec(memory_space=pltpu.SMEM), whole(keys.shape), whole(values.shape)]
        + [of_layer(array, layer) for array in pieces]
        + [whole((4, total))] * len(stats),
        out_specs=[whole(shape) for shape in outs],
        out_shape=[jax.ShapeDtypeStruct(shape, BF16) for shape in outs],
        compiler_params=params(),
        cost_estimate=cost(
            10 * enc_rows * total * size, 6 * size * (enc_rows + total), enc_rows * total
        ),
    )(flip, keys, values, *pieces, *stats)


def back_kernel(order_ref, wk_ref, wv_ref, *refs):
    out = refs[-1]
    layers = wk_ref.shape[0]
    total = refs[2 * layers][0].astype(F32) if len(refs) > 2 * layers + 1 else None
    for layer in range(layers):
        part = dot(refs[2 * layer][...], wk_ref[layer], NT)
        total = part if total is None else total + part
        total = total + dot(refs[2 * layer + 1][...], wv_ref[layer], NT)
    out[0] = total.astype(BF16)


def back_blocks(order, wk, wv, flat, share, arrived=None):
    layers, _, size = wk.shape
    rows = flat[0].shape[0]
    blocks = order.shape[0]
    weight = pl.BlockSpec((layers, share, size), lambda i, order: (0, order[i], 0))
    result = pl.BlockSpec((1, rows, share), lambda i, order: (i, 0, 0))
    extra = [] if arrived is None else [arrived]
    return pl.pallas_call(
        back_kernel,
        grid_spec=pltpu.PrefetchScalarGridSpec(
            num_scalar_prefetch=1,
            grid=(blocks,),
            in_specs=[weight, weight]
            + [pl.BlockSpec((rows, size), lambda i, order: (0, 0))] * len(flat)
            + [result] * len(extra),
            out_specs=result,
        ),
        out_shape=jax.ShapeDtypeStruct((blocks, rows, share), BF16),
        compiler_params=params(),
        cost_estimate=cost(
            4 * layers * rows * size * share * blocks, 2 * blocks * share * (2 * layers * size + 2 * rows)
        ),
    )(order, wk, wv, *flat, *extra)


def plus(one, two):
    return (one.astype(F32) + two.astype(F32)).astype(BF16)


def exchange(value, n_inp, n_tgt, mask_of):
    pairs = [(z * n_tgt + t, z * n_tgt + (t ^ mask_of(z))) for z in range(n_inp) for t in range(n_tgt)]
    return lax.ppermute(value, ("inp", "tgt"), pairs)


def everywhere(value, n_inp):
    return [value] + [
        lax.ppermute(value, "inp", [(i, (i + shift) % n_inp) for i in range(n_inp)])
        for shift in range(1, n_inp)
    ]


def after(value, *others):
    return lax.optimization_barrier((value, *others))[0]


class LineSums:
    def __init__(self, n_inp):
        self.n_inp, self.inner, self.total, self.outer = n_inp, [], [], []

    def send(self, value, *others, hold=()):
        if self.n_inp != 4:
            total = lax.psum(value, "inp")
            self.total.append(total)
            self.outer.append(total)
            return
        count = len(self.total)

        def earlier(results, back):
            return results[count - back : count - back + 1] if count >= back else []

        lead = 1 if count < 2 else 2
        value = after(value, *others, *earlier(self.inner, lead), *earlier(self.total, 3), *earlier(self.outer, 4))
        inner = plus(after(value, *hold), lax.ppermute(value, "inp", [(0, 1), (3, 2)]))
        inner = after(inner, *earlier(self.outer, 3 if count < 4 else 2))
        total = plus(inner, lax.ppermute(inner, "inp", [(1, 2), (2, 1)]))
        total = after(total, *earlier(self.outer, 2))
        self.inner.append(inner)
        self.total.append(total)
        self.outer.append(lax.ppermute(total, "inp", [(1, 0), (2, 3)]))


def body(encoder, key_weight, value_weight, queries, grad_out):
    layers, dec_rows, heads, size = queries.shape
    width = encoder.shape[1]
    n_inp, n_tgt, n_mdl = (lax.axis_size(axis) for axis in ("inp", "tgt", "mdl"))
    z, t, m = (lax.axis_index(axis) for axis in ("inp", "tgt", "mdl"))
    share = width // (n_tgt * n_mdl)
    wk = key_weight.reshape(layers, width, size)
    wv = value_weight.reshape(layers, width, size)
    far = ((z == 0) | (z == n_inp - 1)).astype(jnp.int32)
    odd = (z % 2).astype(jnp.int32)
    rank = jnp.stack([t.astype(jnp.int32), far])

    sources = [jnp.transpose(array, (2, 0, 1, 3)) for array in (queries, grad_out)]

    def head(source, mask):
        return lax.dynamic_index_in_dim(source, t ^ mask, 0, keepdims=False)

    wanted = [[head(source, 2 + odd)[layer : layer + 1] for source in sources] for layer in range(layers)]
    fetched = [
        [exchange(piece, n_inp, n_tgt, lambda z: 2 + z % 2) for piece in pair] for pair in wanted
    ]
    own = [head(source, 0) for source in sources]
    beside = [lax.ppermute(head(source, 1), "tgt", partners(n_tgt, 1)) for source in sources]
    begun = [piece for pair in wanted for piece in pair]
    keys, values, handed = [], [], []
    for layer in range(layers):
        key_block, value_block = project(after(encoder, *begun), wk, wv, layer)
        begun = fetched[0][:1]
        keys.append(key_block)
        values.append(value_block)
    for layer in range(layers):
        handed.append([])
        for kind in range(2):
            ahead = keys[min(layers - 1, 2 * layer + kind)]
            handed[layer].append(lax.ppermute(after(fetched[layer][kind], ahead), "inp", partners(n_inp, 1)))

    pieces, stats = [], []
    for layer in range(layers):
        pieces.append(
            [
                array
                for kind in range(2)
                for array in (own[kind], beside[kind], fetched[layer][kind], handed[layer][kind])
            ]
        )
        own_stats = row_stats(odd[None], keys[layer], values[layer], pieces[layer], layer)
        stats.append(everywhere(own_stats, n_inp))
    flat, near, straight, across = [], [], [], []
    for layer in range(layers):
        results = attention_grads(odd[None], keys[layer], values[layer], pieces[layer], stats[layer], layer)
        near.append(results[0])
        straight.append(lax.ppermute(after(results[1], *straight[-1:]), "tgt", partners(n_tgt, 2)))
        across.append(lax.ppermute(after(results[2], *across[-1:]), "tgt", partners(n_tgt, 3)))
        flat += results[3:]
    sums_over = LineSums(n_inp)
    for layer in range(layers):
        sums_over.send(near[layer], *(stats[-1] if layer == 0 else ()), hold=near[-1:])

    def order(mask):
        return jnp.stack([(t ^ mask) * n_mdl + (m ^ side) for side in range(n_mdl)]).astype(jnp.int32)

    masks = list(reversed(range(0, n_tgt, 2)))
    arrived = []
    for mask in masks:
        sent = back_blocks(after(order(mask + 1), across[0]), wk, wv, flat, share)
        arrived.append(lax.ppermute(sent, "tgt", partners(n_tgt, 1)))
    sums_over.send(straight[0])
    total, blocks = None, []
    for mask, wait, block in zip(masks, [straight[-1], across[-1]], arrived):
        blocks.append(back_blocks(after(order(mask), wait), wk, wv, flat, share, block))
        for side in reversed(range(n_mdl)):
            block = blocks[-1][side]
            if mask or side:
                pairs = [
                    (a * n_mdl + b, (a ^ mask) * n_mdl + (b ^ side))
                    for a in range(n_tgt)
                    for b in range(n_mdl)
                ]
                block = lax.ppermute(block, ("tgt", "mdl"), pairs)
            total = block.astype(F32) if total is None else total + block.astype(F32)
    later = [piece for pair in zip(straight, across) for piece in pair][1:]
    for index, piece in enumerate(later):
        sums_over.send(piece, *blocks[index : index + 1])
    done = list(zip(sums_over.total, sums_over.outer))
    beside_grad = jnp.stack([jnp.where(far > 0, there[1], here[1]) for here, there in done[:layers]])
    beside_grad = lax.ppermute(beside_grad, "tgt", partners(n_tgt, 1))
    query_grads = None
    for layer in range(layers):
        chunks = [done[layer], (beside_grad,) * 2, done[layers + 2 * layer], done[layers + 2 * layer + 1]]
        places = [(chunk[side], layer if mask == 1 else 0) for side in range(2) for mask, chunk in enumerate(chunks)]
        query_grads = join_heads(rank, places, layer, layers, query_grads)

    return query_grads, total.astype(BF16)


def solution(mesh):
    placed = (
        P("inp", None),
        P(None, None, "mdl", "tgt", None),
        P(None, None, "mdl", "tgt", None),
        P(None, "tgt", "mdl", None),
        P(None, "tgt", "mdl", None),
    )
    return jax.shard_map(
        body,
        mesh=mesh,
        in_specs=placed,
        out_specs=(P(None, "tgt", "mdl", None), P("inp", ("tgt", "mdl"))),
        check_vma=False,
    )
```

```python
import functools

import jax
import jax.numpy as jnp
from jax import lax
from jax.experimental import pallas as pl
from jax.experimental.pallas import tpu as pltpu
from jax.sharding import PartitionSpec as P

F32, BF16 = jnp.float32, jnp.bfloat16
MIB = 1024 * 1024
NT = (((1,), (1,)), ((), ()))
NN = (((1,), (0,)), ((), ()))
TN = (((0,), (0,)), ((), ()))


def dot(left, right, dims):
    return lax.dot_general(left, right, dims, preferred_element_type=F32)


def params():
    return pltpu.CompilerParams(vmem_limit_bytes=44 * MIB)


def cost(flops, nbytes, exps=0):
    return pl.CostEstimate(flops=int(flops), bytes_accessed=int(nbytes), transcendentals=int(exps))


def partners(count, mask):
    return [(index, index ^ mask) for index in range(count)]


def pick_kernel(head_ref, *refs):
    count = len(refs) // 2
    for source, out in zip(refs[:count], refs[count:]):
        out[...] = source[0]


def pick(head, parts):
    shape = parts[0][0].shape
    specs, outs = [], []
    for source, first, count in parts:
        specs.append(
            pl.BlockSpec((1, count) + shape[2:], lambda i, head, first=first: (head[0], first, 0, 0))
        )
        outs.append(jax.ShapeDtypeStruct((count,) + shape[2:], BF16))
    return pl.pallas_call(
        pick_kernel,
        grid_spec=pltpu.PrefetchScalarGridSpec(
            num_scalar_prefetch=1,
            grid=(1,),
            in_specs=specs,
            out_specs=[pl.BlockSpec(out.shape, lambda i, head: (0, 0, 0)) for out in outs],
        ),
        out_shape=outs,
        compiler_params=params(),
        cost_estimate=cost(0, 4 * sum(out.size for out in outs)),
    )(head, *[source for source, _, _ in parts])


def join_kernel(place_ref, mine_ref, other_ref, *rest):
    out = rest[-1]
    heads, half, _ = mine_ref.shape

    def fill(upper_ref, lower_ref):
        for head in range(heads):
            out[0, :half, head, :] = upper_ref[place_ref[0] ^ head]
            out[0, half:, head, :] = lower_ref[place_ref[0] ^ head]

    pl.when(place_ref[2] != 0)(lambda: fill(mine_ref, other_ref))
    pl.when(place_ref[2] == 0)(lambda: fill(other_ref, mine_ref))


def join_heads(place, mine, other, layer, layers, begun):
    heads, half, size = mine.shape
    extra = [] if begun is None else [begun]
    return pl.pallas_call(
        join_kernel,
        grid_spec=pltpu.PrefetchScalarGridSpec(
            num_scalar_prefetch=1,
            grid=(1,),
            in_specs=[whole(mine.shape)] * 2 + [pl.BlockSpec(memory_space=pl.ANY)] * len(extra),
            out_specs=pl.BlockSpec((1, 2 * half, heads, size), lambda i, place: (layer, 0, 0, 0)),
        ),
        out_shape=jax.ShapeDtypeStruct((layers, 2 * half, heads, size), BF16),
        input_output_aliases={3: 0} if extra else {},
        compiler_params=params(),
        cost_estimate=cost(0, 8 * half * heads * size),
    )(place, mine, other, *extra)


def project_kernel(enc_ref, wk_ref, wv_ref, k_ref, v_ref, sums):
    step = pl.program_id(0)

    @pl.when(step == 0)
    def _():
        sums[...] = jnp.zeros_like(sums)

    sums[0] += dot(enc_ref[...], wk_ref[0], NN)
    sums[1] += dot(enc_ref[...], wv_ref[0], NN)

    @pl.when(step == pl.num_programs(0) - 1)
    def _():
        k_ref[...] = sums[0].astype(BF16)
        v_ref[...] = sums[1].astype(BF16)


def project(encoder, wk, wv, layer):
    rows, width = encoder.shape
    size = wk.shape[2]
    depth = width // 4
    weight = pl.BlockSpec((1, depth, size), lambda i: (layer, i, 0))
    result = pl.BlockSpec((rows, size), lambda i: (0, 0))
    return pl.pallas_call(
        project_kernel,
        grid=(width // depth,),
        in_specs=[pl.BlockSpec((rows, depth), lambda i: (0, i)), weight, weight],
        out_specs=[result, result],
        out_shape=[jax.ShapeDtypeStruct((rows, size), BF16)] * 2,
        scratch_shapes=[pltpu.VMEM((2, rows, size), F32)],
        compiler_params=params(),
        cost_estimate=cost(4 * rows * width * size, 2 * width * (rows + 2 * size)),
    )(encoder, wk, wv)


def columns(index, count, rows, place_ref):
    if index < count - 2:
        return slice(index * rows, (index + 1) * rows)
    start = (count - 2 + ((index - count + 2) ^ place_ref[1])) * rows
    return pl.ds(pl.multiple_of(start, rows), rows)


def block_of(ref):
    return ref[(0,) * (len(ref.shape) - 2)]


def stats_kernel(place_ref, k_ref, v_ref, *refs):
    out, pieces = refs[-1], refs[:-1]
    count = len(pieces) // 2
    for index in range(count):
        query, cotangent = block_of(pieces[index]), block_of(pieces[count + index])
        cols = columns(index, count, query.shape[0], place_ref)
        scores = dot(k_ref[...], query, NT)
        peak = jnp.max(scores, axis=0, keepdims=True)
        shifted = jnp.exp(scores - peak)
        dprobs = dot(v_ref[...], cotangent, NT)
        out[0:1, cols] = peak
        out[1:2, cols] = jnp.sum(shifted, axis=0, keepdims=True)
        out[2:3, cols] = jnp.sum(shifted * dprobs, axis=0, keepdims=True)
        out[3:4, cols] = jnp.zeros_like(peak)


def whole(shape):
    return pl.BlockSpec(shape, lambda i, *place: (0,) * len(shape))


def of_layer(array, layer):
    if len(array.shape) == 4:
        return pl.BlockSpec((1, 1) + array.shape[2:], lambda i, place: (place[0], layer, 0, 0))
    index = layer if array.shape[0] > 1 else 0
    return pl.BlockSpec((1,) + array.shape[1:], lambda i, place: (index, 0, 0))


def row_stats(place, keys, values, pieces, layer):
    enc_rows, size = keys.shape
    total = pieces[0].shape[-2] * len(pieces) // 2
    return pl.pallas_call(
        stats_kernel,
        grid_spec=pltpu.PrefetchScalarGridSpec(
            num_scalar_prefetch=1,
            grid=(1,),
            in_specs=[whole(keys.shape), whole(values.shape)] + [of_layer(array, layer) for array in pieces],
            out_specs=whole((4, total)),
        ),
        out_shape=jax.ShapeDtypeStruct((4, total), F32),
        compiler_params=params(),
        cost_estimate=cost(
            4 * enc_rows * total * size, 4 * size * (enc_rows + total), enc_rows * total
        ),
    )(place, keys, values, *pieces)


def grads_kernel(count, place_ref, k_ref, v_ref, *refs):
    queries, cotangents, refs = refs[:count], refs[count : 2 * count], refs[2 * count :]
    stats, (keep_ref, send_ref, dk_ref, dv_ref) = refs[:-4], refs[-4:]
    keys, values = k_ref[...], v_ref[...]
    half = keep_ref.shape[1]
    for index in range(count):
        query, cotangent = block_of(queries[index]), block_of(cotangents[index])
        cols = columns(index, count, query.shape[0], place_ref)
        parts = [part[:, cols] for part in stats]
        peak = functools.reduce(jnp.maximum, [part[0:1] for part in parts])
        scales = [jnp.exp(part[0:1] - peak) for part in parts]
        total = sum(part[1:2] * scale for part, scale in zip(parts, scales))
        inner = sum(part[2:3] * scale for part, scale in zip(parts, scales)) / total
        attention = jnp.exp(dot(keys, query, NT) - peak) * (1.0 / total)
        dprobs = dot(values, cotangent, NT)
        dscores = (attention * (dprobs - inner)).astype(BF16)
        query_grad = dot(dscores, keys, TN).astype(BF16)
        slot = index if index < count - 2 else count - 2 + ((index - count + 2) ^ place_ref[1])
        upper, lower = query_grad[:half], query_grad[half:]
        first = place_ref[2] != 0
        keep_ref[slot] = jnp.where(first, upper, lower)
        send_ref[slot] = jnp.where(first, lower, upper)
        key_part = dot(dscores, query, NN)
        value_part = dot(attention.astype(BF16), cotangent, NN)
        key_sum = key_part if index == 0 else key_sum + key_part
        value_sum = value_part if index == 0 else value_sum + value_part
    dk_ref[...] = key_sum.astype(BF16)
    dv_ref[...] = value_sum.astype(BF16)


def attention_grads(place, keys, values, pieces, stats, layer):
    enc_rows, size = keys.shape
    rows = pieces[0].shape[-2]
    count = len(pieces) // 2
    total = rows * count
    outs = [(count, rows // 2, size)] * 2 + [(enc_rows, size)] * 2
    return pl.pallas_call(
        functools.partial(grads_kernel, count),
        grid_spec=pltpu.PrefetchScalarGridSpec(
            num_scalar_prefetch=1,
            grid=(1,),
            in_specs=[whole(keys.shape), whole(values.shape)]
            + [of_layer(array, layer) for array in pieces]
            + [whole((4, total))] * len(stats),
            out_specs=[whole(shape) for shape in outs],
        ),
        out_shape=[jax.ShapeDtypeStruct(shape, BF16) for shape in outs],
        compiler_params=params(),
        cost_estimate=cost(
            10 * enc_rows * total * size, 6 * size * (enc_rows + total), enc_rows * total
        ),
    )(place, keys, values, *pieces, *stats)


def back_kernel(order_ref, wk_ref, wv_ref, *refs):
    out = refs[-1]
    layers = wk_ref.shape[0]
    total = refs[2 * layers][0].astype(F32) if len(refs) > 2 * layers + 1 else None
    for layer in range(layers):
        part = dot(refs[2 * layer][...], wk_ref[layer], NT)
        total = part if total is None else total + part
        total = total + dot(refs[2 * layer + 1][...], wv_ref[layer], NT)
    out[0] = total.astype(BF16)


def back_blocks(order, wk, wv, flat, share, arrived=None):
    layers, _, size = wk.shape
    rows = flat[0].shape[0]
    blocks = order.shape[0]
    weight = pl.BlockSpec((layers, share, size), lambda i, order: (0, order[i], 0))
    result = pl.BlockSpec((1, rows, share), lambda i, order: (i, 0, 0))
    extra = [] if arrived is None else [arrived]
    return pl.pallas_call(
        back_kernel,
        grid_spec=pltpu.PrefetchScalarGridSpec(
            num_scalar_prefetch=1,
            grid=(blocks,),
            in_specs=[weight, weight]
            + [pl.BlockSpec((rows, size), lambda i, order: (0, 0))] * len(flat)
            + [result] * len(extra),
            out_specs=result,
        ),
        out_shape=jax.ShapeDtypeStruct((blocks, rows, share), BF16),
        compiler_params=params(),
        cost_estimate=cost(
            4 * layers * rows * size * share * blocks, 2 * blocks * share * (2 * layers * size + 2 * rows)
        ),
    )(order, wk, wv, *flat, *extra)


def plus(one, two):
    return (one.astype(F32) + two.astype(F32)).astype(BF16)


def exchange(value, n_inp, n_tgt, mask_of):
    pairs = [(z * n_tgt + t, z * n_tgt + (t ^ mask_of(z))) for z in range(n_inp) for t in range(n_tgt)]
    return lax.ppermute(value, ("inp", "tgt"), pairs)


def everywhere(value, n_inp):
    return [value] + [
        lax.ppermute(value, "inp", [(i, (i + shift) % n_inp) for i in range(n_inp)])
        for shift in range(1, n_inp)
    ]


def after(value, *others):
    return lax.optimization_barrier((value, *others))[0]


def to_owners(value, n_tgt):
    return jnp.stack(
        [
            value[mask] if mask == 0 else lax.ppermute(value[mask], "tgt", partners(n_tgt, mask))
            for mask in range(n_tgt)
        ]
    )


def body(encoder, key_weight, value_weight, queries, grad_out):
    layers, dec_rows, heads, size = queries.shape
    width = encoder.shape[1]
    n_inp, n_tgt, n_mdl = (lax.axis_size(axis) for axis in ("inp", "tgt", "mdl"))
    z, t, m = (lax.axis_index(axis) for axis in ("inp", "tgt", "mdl"))
    share = width // (n_tgt * n_mdl)
    wk = key_weight.reshape(layers, width, size)
    wv = value_weight.reshape(layers, width, size)
    line = n_inp == 4
    odd = (z % 2).astype(jnp.int32)
    upper = ((z == 0) | (z == n_inp - 1)).astype(jnp.int32) if line else jnp.ones_like(odd)
    place = jnp.stack([t.astype(jnp.int32), odd, upper])

    own = [jnp.transpose(array, (2, 0, 1, 3)) for array in (queries, grad_out)]
    wanted = pick((t ^ (2 + odd))[None], [(source, layer, 1) for layer in range(layers) for source in own])
    fetched = [exchange(piece, n_inp, n_tgt, lambda z: 2 + z % 2) for piece in wanted]
    keys, values, begun = [], [], wanted
    for layer in range(layers):
        key_block, value_block = project(after(encoder, *begun), wk, wv, layer)
        begun = fetched[:1]
        keys.append(key_block)
        values.append(value_block)
    beside = pick(after((t ^ 1)[None], keys[0]), [(source, 0, layers) for source in own])
    beside = [lax.ppermute(piece, "tgt", partners(n_tgt, 1)) for piece in beside]
    handed = []
    for index, piece in enumerate(fetched):
        ahead = keys[min(layers - 1, index)]
        handed.append(lax.ppermute(after(piece, ahead), "inp", partners(n_inp, 1)))

    pieces, stats = [], []
    for layer in range(layers):
        pieces.append(
            [
                array
                for kind in range(2)
                for array in (own[kind], beside[kind], fetched[2 * layer + kind], handed[2 * layer + kind])
            ]
        )
        own_stats = row_stats(place, keys[layer], values[layer], pieces[layer], layer)
        stats.append(everywhere(own_stats, n_inp))
    flat, keep, send = [], [], []
    for layer in range(layers):
        results = attention_grads(place, keys[layer], values[layer], pieces[layer], stats[layer], layer)
        keep.append(results[0])
        send.append(results[1])
        flat += results[2:]

    def order(mask):
        return jnp.stack([(t ^ mask) * n_mdl + (m ^ side) for side in range(n_mdl)]).astype(jnp.int32)

    def pair_sum(layer, *others):
        value = after(send[layer], *stats[-1]) if layer == 0 else send[layer]
        return plus(after(keep[layer], *others), lax.ppermute(value, "inp", partners(n_inp, 1)))

    pair_sums = [pair_sum(0, flat[-1])] if line else []
    masks = list(reversed(range(0, n_tgt, 2)))
    arrived = []
    for index, mask in enumerate(masks):
        wait = pair_sums if index else []
        sent = back_blocks(after(order(mask + 1), *wait), wk, wv, flat, share)
        arrived.append(lax.ppermute(sent, "tgt", partners(n_tgt, 1)))
    total, blocks = None, keys[0]
    for mask, block in zip(masks, arrived):
        blocks = back_blocks(after(order(mask), blocks), wk, wv, flat, share, block)
        for side in reversed(range(n_mdl)):
            block = blocks[side]
            if mask or side:
                pairs = [
                    (a * n_mdl + b, (a ^ mask) * n_mdl + (b ^ side))
                    for a in range(n_tgt)
                    for b in range(n_mdl)
                ]
                block = lax.ppermute(block, ("tgt", "mdl"), pairs)
            total = block.astype(F32) if total is None else total + block.astype(F32)

    query_grads = None
    if line:
        pair_sums += [pair_sum(layer, blocks) for layer in range(1, layers)]
        opposite = [(0, 3), (3, 0), (1, 2), (2, 1)]
        mine = [to_owners(plus(value, lax.ppermute(value, "inp", opposite)), n_tgt) for value in pair_sums]
        other = [lax.ppermute(value, "inp", partners(n_inp, 1)) for value in mine]
    else:
        mine, other = ([to_owners(lax.psum(value, "inp"), n_tgt) for value in half] for half in (keep, send))
    for layer in range(layers):
        query_grads = join_heads(place, mine[layer], other[layer], layer, layers, query_grads)
    return query_grads, total.astype(BF16)


def solution(mesh):
    placed = (
        P("inp", None),
        P(None, None, "mdl", "tgt", None),
        P(None, None, "mdl", "tgt", None),
        P(None, "tgt", "mdl", None),
        P(None, "tgt", "mdl", None),
    )
    return jax.shard_map(
        body,
        mesh=mesh,
        in_specs=placed,
        out_specs=(P(None, "tgt", "mdl", None), P("inp", ("tgt", "mdl"))),
        check_vma=False,
    )
```

```python
import functools

import jax
import jax.numpy as jnp
from jax import lax
from jax.experimental import pallas as pl
from jax.experimental.pallas import tpu as pltpu
from jax.sharding import PartitionSpec as P

F32, BF16 = jnp.float32, jnp.bfloat16
MIB = 1024 * 1024
NT = (((1,), (1,)), ((), ()))
NN = (((1,), (0,)), ((), ()))
TN = (((0,), (0,)), ((), ()))


def dot(left, right, dims):
    return lax.dot_general(left, right, dims, preferred_element_type=F32)


def params():
    return pltpu.CompilerParams(vmem_limit_bytes=24 * MIB)


def cost(flops, nbytes, exps=0):
    return pl.CostEstimate(flops=int(flops), bytes_accessed=int(nbytes), transcendentals=int(exps))


def in_hbm(*arrays):
    return [pltpu.with_memory_space_constraint(array, pltpu.HBM) for array in arrays]


def partners(count, mask):
    return [(index, index ^ mask) for index in range(count)]


def pick_kernel(head_ref, *refs):
    count = len(refs) // 2
    for source, out in zip(refs[:count], refs[count:]):
        out[...] = source[0]


def pick(head, parts):
    shape = parts[0][0].shape
    specs, outs = [], []
    for source, first, count in parts:
        specs.append(
            pl.BlockSpec((1, count) + shape[2:], lambda i, head, first=first: (head[0], first, 0, 0))
        )
        outs.append(jax.ShapeDtypeStruct((count,) + shape[2:], BF16))
    return pl.pallas_call(
        pick_kernel,
        grid_spec=pltpu.PrefetchScalarGridSpec(
            num_scalar_prefetch=1,
            grid=(1,),
            in_specs=specs,
            out_specs=[pl.BlockSpec(out.shape, lambda i, head: (0, 0, 0)) for out in outs],
        ),
        out_shape=outs,
        compiler_params=params(),
        cost_estimate=cost(0, 4 * sum(out.size for out in outs)),
    )(head, *[source for source, _, _ in parts])


def join_kernel(place_ref, mine_ref, other_ref, *rest):
    out = rest[-1]
    heads, half, _ = mine_ref.shape

    def fill(upper_ref, lower_ref):
        for head in range(heads):
            out[0, :half, head, :] = upper_ref[place_ref[0] ^ head]
            out[0, half:, head, :] = lower_ref[place_ref[0] ^ head]

    pl.when(place_ref[2] != 0)(lambda: fill(mine_ref, other_ref))
    pl.when(place_ref[2] == 0)(lambda: fill(other_ref, mine_ref))


def join_heads(place, mine, other, layer, layers, begun):
    heads, half, size = mine.shape
    extra = [] if begun is None else [begun]
    return pl.pallas_call(
        join_kernel,
        grid_spec=pltpu.PrefetchScalarGridSpec(
            num_scalar_prefetch=1,
            grid=(1,),
            in_specs=[whole(mine.shape)] * 2 + [pl.BlockSpec(memory_space=pl.ANY)] * len(extra),
            out_specs=pl.BlockSpec((1, 2 * half, heads, size), lambda i, place: (layer, 0, 0, 0)),
        ),
        out_shape=jax.ShapeDtypeStruct((layers, 2 * half, heads, size), BF16),
        input_output_aliases={3: 0} if extra else {},
        compiler_params=params(),
        cost_estimate=cost(0, 8 * half * heads * size),
    )(place, mine, other, *extra)


def project_kernel(enc_ref, wk_ref, wv_ref, k_ref, v_ref, sums):
    step = pl.program_id(0)

    @pl.when(step == 0)
    def _():
        sums[...] = jnp.zeros_like(sums)

    sums[0] += dot(enc_ref[...], wk_ref[0], NN)
    sums[1] += dot(enc_ref[...], wv_ref[0], NN)

    @pl.when(step == pl.num_programs(0) - 1)
    def _():
        k_ref[...] = sums[0].astype(BF16)
        v_ref[...] = sums[1].astype(BF16)


def project(encoder, wk, wv, layer):
    rows, width = encoder.shape
    size = wk.shape[2]
    depth = width // 4
    weight = pl.BlockSpec((1, depth, size), lambda i: (layer, i, 0))
    result = pl.BlockSpec((rows, size), lambda i: (0, 0))
    return pl.pallas_call(
        project_kernel,
        grid=(width // depth,),
        in_specs=[pl.BlockSpec((rows, depth), lambda i: (0, i)), weight, weight],
        out_specs=[result, result],
        out_shape=[jax.ShapeDtypeStruct((rows, size), BF16)] * 2,
        scratch_shapes=[pltpu.VMEM((2, rows, size), F32)],
        compiler_params=params(),
        cost_estimate=cost(4 * rows * width * size, 2 * width * (rows + 2 * size)),
    )(*in_hbm(encoder, wk, wv))


def columns(index, count, rows, place_ref):
    if index < count - 2:
        return slice(index * rows, (index + 1) * rows)
    start = (count - 2 + ((index - count + 2) ^ place_ref[1])) * rows
    return pl.ds(pl.multiple_of(start, rows), rows)


def block_of(ref):
    return ref[(0,) * (len(ref.shape) - 2)]


def stats_kernel(place_ref, k_ref, v_ref, *refs):
    out, pieces = refs[-1], refs[:-1]
    count = len(pieces) // 2
    for index in range(count):
        query, cotangent = block_of(pieces[index]), block_of(pieces[count + index])
        cols = columns(index, count, query.shape[0], place_ref)
        scores = dot(k_ref[...], query, NT)
        peak = jnp.max(scores, axis=0, keepdims=True)
        shifted = jnp.exp(scores - peak)
        dprobs = dot(v_ref[...], cotangent, NT)
        out[0:1, cols] = peak
        out[1:2, cols] = jnp.sum(shifted, axis=0, keepdims=True)
        out[2:3, cols] = jnp.sum(shifted * dprobs, axis=0, keepdims=True)
        out[3:4, cols] = jnp.zeros_like(peak)


def whole(shape):
    return pl.BlockSpec(shape, lambda i, *place: (0,) * len(shape))


def of_layer(array, layer):
    if len(array.shape) == 4:
        return pl.BlockSpec((1, 1) + array.shape[2:], lambda i, place: (place[0], layer, 0, 0))
    index = layer if array.shape[0] > 1 else 0
    return pl.BlockSpec((1,) + array.shape[1:], lambda i, place: (index, 0, 0))


def row_stats(place, keys, values, pieces, layer):
    enc_rows, size = keys.shape
    total = pieces[0].shape[-2] * len(pieces) // 2
    return pl.pallas_call(
        stats_kernel,
        grid_spec=pltpu.PrefetchScalarGridSpec(
            num_scalar_prefetch=1,
            grid=(1,),
            in_specs=[whole(keys.shape), whole(values.shape)] + [of_layer(array, layer) for array in pieces],
            out_specs=whole((4, total)),
        ),
        out_shape=jax.ShapeDtypeStruct((4, total), F32),
        compiler_params=params(),
        cost_estimate=cost(
            4 * enc_rows * total * size, 4 * size * (enc_rows + total), enc_rows * total
        ),
    )(place, keys, values, *pieces)


def grads_kernel(count, place_ref, k_ref, v_ref, *refs):
    queries, cotangents, refs = refs[:count], refs[count : 2 * count], refs[2 * count :]
    stats, (keep_ref, send_ref, dk_ref, dv_ref) = refs[:-4], refs[-4:]
    keys, values = k_ref[...], v_ref[...]
    half = keep_ref.shape[1]
    for index in range(count):
        query, cotangent = block_of(queries[index]), block_of(cotangents[index])
        cols = columns(index, count, query.shape[0], place_ref)
        parts = [part[:, cols] for part in stats]
        peak = functools.reduce(jnp.maximum, [part[0:1] for part in parts])
        scales = [jnp.exp(part[0:1] - peak) for part in parts]
        total = sum(part[1:2] * scale for part, scale in zip(parts, scales))
        inner = sum(part[2:3] * scale for part, scale in zip(parts, scales)) / total
        attention = jnp.exp(dot(keys, query, NT) - peak) * (1.0 / total)
        dprobs = dot(values, cotangent, NT)
        dscores = (attention * (dprobs - inner)).astype(BF16)
        query_grad = dot(dscores, keys, TN).astype(BF16)
        slot = index if index < count - 2 else count - 2 + ((index - count + 2) ^ place_ref[1])
        upper, lower = query_grad[:half], query_grad[half:]
        first = place_ref[2] != 0
        keep_ref[slot] = jnp.where(first, upper, lower)
        send_ref[slot] = jnp.where(first, lower, upper)
        key_part = dot(dscores, query, NN)
        value_part = dot(attention.astype(BF16), cotangent, NN)
        key_sum = key_part if index == 0 else key_sum + key_part
        value_sum = value_part if index == 0 else value_sum + value_part
    dk_ref[...] = key_sum.astype(BF16)
    dv_ref[...] = value_sum.astype(BF16)


def attention_grads(place, keys, values, pieces, stats, layer):
    enc_rows, size = keys.shape
    rows = pieces[0].shape[-2]
    count = len(pieces) // 2
    total = rows * count
    outs = [(count, rows // 2, size)] * 2 + [(enc_rows, size)] * 2
    return pl.pallas_call(
        functools.partial(grads_kernel, count),
        grid_spec=pltpu.PrefetchScalarGridSpec(
            num_scalar_prefetch=1,
            grid=(1,),
            in_specs=[whole(keys.shape), whole(values.shape)]
            + [of_layer(array, layer) for array in pieces]
            + [whole((4, total))] * len(stats),
            out_specs=[whole(shape) for shape in outs],
        ),
        out_shape=[jax.ShapeDtypeStruct(shape, BF16) for shape in outs],
        compiler_params=params(),
        cost_estimate=cost(
            10 * enc_rows * total * size, 6 * size * (enc_rows + total), enc_rows * total
        ),
    )(place, keys, values, *pieces, *stats)


def back_kernel(added, order_ref, wk_ref, wv_ref, *refs):
    layers = wk_ref.shape[0]
    outs = refs[2 * layers + added :]
    total = refs[2 * layers][0].astype(F32) if added else None
    for layer in range(layers):
        part = dot(refs[2 * layer][...], wk_ref[layer], NT)
        total = part if total is None else total + part
        total = total + dot(refs[2 * layer + 1][...], wv_ref[layer], NT)
    if len(outs) == 1:
        outs[0][0] = total.astype(BF16)
    for index, out in enumerate(outs if len(outs) > 1 else ()):

        @pl.when(pl.program_id(0) == index)
        def _():
            out[0] = total.astype(BF16)


def back_blocks(order, wk, wv, flat, share, arrived=None):
    layers, _, size = wk.shape
    rows = flat[0].shape[0]
    blocks = order.shape[0]
    weight = pl.BlockSpec((layers, share, size), lambda i, order: (0, order[i], 0))
    result = pl.BlockSpec((1, rows, share), lambda i, order: (i, 0, 0))
    extra = [] if arrived is None else [arrived]
    if extra:
        out_specs = [pl.BlockSpec((1, rows, share), lambda i, order: (0, 0, 0))] * blocks
        outs = [jax.ShapeDtypeStruct((1, rows, share), BF16)] * blocks
    else:
        out_specs, outs = result, jax.ShapeDtypeStruct((blocks, rows, share), BF16)
    return pl.pallas_call(
        functools.partial(back_kernel, len(extra)),
        grid_spec=pltpu.PrefetchScalarGridSpec(
            num_scalar_prefetch=1,
            grid=(blocks,),
            in_specs=[weight, weight]
            + [pl.BlockSpec((rows, size), lambda i, order: (0, 0))] * len(flat)
            + [result] * len(extra),
            out_specs=out_specs,
        ),
        out_shape=outs,
        compiler_params=params(),
        cost_estimate=cost(
            4 * layers * rows * size * share * blocks, 2 * blocks * share * (2 * layers * size + 2 * rows)
        ),
    )(order, *in_hbm(wk, wv), *flat, *extra)


def plus_kernel(one_ref, two_ref, *outs):
    total = (one_ref[...].astype(F32) + two_ref[...].astype(F32)).astype(BF16)
    for index, out in enumerate(outs):
        out[...] = total if len(outs) == 1 else total[index]


def plus(one, two, spread=False):
    shape = one.shape[1:] if spread else one.shape
    outs = [jax.ShapeDtypeStruct(shape, BF16)] * (one.shape[0] if spread else 1)
    results = pl.pallas_call(
        plus_kernel,
        grid=(1,),
        in_specs=[whole(one.shape)] * 2,
        out_specs=[whole(shape)] * len(outs),
        out_shape=outs,
        compiler_params=params(),
        cost_estimate=cost(one.size, 6 * one.size),
    )(one, two)
    return results if spread else results[0]


def stack_kernel(*refs):
    for index, ref in enumerate(refs[:-1]):
        refs[-1][index] = ref[...]


def stacked(parts):
    shape = (len(parts),) + parts[0].shape
    return pl.pallas_call(
        stack_kernel,
        grid=(1,),
        in_specs=[whole(parts[0].shape)] * len(parts),
        out_specs=whole(shape),
        out_shape=jax.ShapeDtypeStruct(shape, BF16),
        compiler_params=params(),
        cost_estimate=cost(0, 4 * len(parts) * parts[0].size),
    )(*parts)


def total_kernel(*refs):
    total = refs[0][0].astype(F32)
    for ref in refs[1:-1]:
        total = total + ref[0].astype(F32)
    refs[-1][...] = total.astype(BF16)


def total_of(parts):
    shape = parts[0].shape[1:]
    return pl.pallas_call(
        total_kernel,
        grid=(1,),
        in_specs=[whole(parts[0].shape)] * len(parts),
        out_specs=whole(shape),
        out_shape=jax.ShapeDtypeStruct(shape, BF16),
        compiler_params=params(),
        cost_estimate=cost(len(parts) * parts[0].size, 2 * (len(parts) + 1) * parts[0].size),
    )(*parts)


def exchange(value, n_inp, n_tgt, mask_of):
    pairs = [(z * n_tgt + t, z * n_tgt + (t ^ mask_of(z))) for z in range(n_inp) for t in range(n_tgt)]
    return lax.ppermute(value, ("inp", "tgt"), pairs)


def everywhere(value, n_inp):
    return [value] + [
        lax.ppermute(value, "inp", [(i, (i + shift) % n_inp) for i in range(n_inp)])
        for shift in range(1, n_inp)
    ]


def after(value, *others):
    return lax.optimization_barrier((value, *others))[0]


def to_owners(parts, n_tgt):
    return stacked(
        [part if mask == 0 else lax.ppermute(part, "tgt", partners(n_tgt, mask)) for mask, part in enumerate(parts)]
    )


def body(encoder, key_weight, value_weight, queries, grad_out):
    layers, dec_rows, heads, size = queries.shape
    width = encoder.shape[1]
    n_inp, n_tgt, n_mdl = (lax.axis_size(axis) for axis in ("inp", "tgt", "mdl"))
    z, t, m = (lax.axis_index(axis) for axis in ("inp", "tgt", "mdl"))
    share = width // (n_tgt * n_mdl)
    wk = key_weight.reshape(layers, width, size)
    wv = value_weight.reshape(layers, width, size)
    line = n_inp == 4
    odd = (z % 2).astype(jnp.int32)
    upper = ((z == 0) | (z == n_inp - 1)).astype(jnp.int32) if line else jnp.ones_like(odd)
    place = jnp.stack([t.astype(jnp.int32), odd, upper])
    wanted_head, beside_head = (t ^ (2 + odd))[None], (t ^ 1)[None]
    orders = [
        jnp.stack([(t ^ mask) * n_mdl + (m ^ side) for side in range(n_mdl)]).astype(jnp.int32)
        for mask in range(n_tgt)
    ]
    queries, place, wanted_head, beside_head, *orders = lax.optimization_barrier(
        (queries, place, wanted_head, beside_head, *orders)
    )

    own = [jnp.transpose(array, (2, 0, 1, 3)) for array in (queries, grad_out)]
    wanted = pick(wanted_head, [(source, layer, 1) for layer in range(layers) for source in own])
    fetched = [exchange(piece, n_inp, n_tgt, lambda z: 2 + z % 2) for piece in wanted]
    keys, values, begun = [], [], wanted
    for layer in range(layers):
        key_block, value_block = project(after(encoder, *begun), wk, wv, layer)
        begun = fetched[:1]
        keys.append(key_block)
        values.append(value_block)
    beside = pick(after(beside_head, keys[0]), [(source, 0, layers) for source in own])
    beside = [lax.ppermute(piece, "tgt", partners(n_tgt, 1)) for piece in beside]
    handed = []
    for index, piece in enumerate(fetched):
        ahead = keys[min(layers - 1, index)]
        handed.append(lax.ppermute(after(piece, ahead), "inp", partners(n_inp, 1)))

    pieces, stats = [], []
    for layer in range(layers):
        pieces.append(
            [
                array
                for kind in range(2)
                for array in (own[kind], beside[kind], fetched[2 * layer + kind], handed[2 * layer + kind])
            ]
        )
        own_stats = row_stats(place, keys[layer], values[layer], pieces[layer], layer)
        stats.append(everywhere(own_stats, n_inp))
    flat, keep, send = [], [], []
    for layer in range(layers):
        results = attention_grads(place, keys[layer], values[layer], pieces[layer], stats[layer], layer)
        keep.append(results[0])
        send.append(results[1])
        flat += results[2:]

    def pair_sum(layer, *others):
        value = after(send[layer], *stats[-1]) if layer == 0 else send[layer]
        return plus(after(keep[layer], *others), lax.ppermute(value, "inp", partners(n_inp, 1)))

    pair_sums = [pair_sum(0, flat[-1])] if line else []
    masks = list(reversed(range(0, n_tgt, 2)))
    arrived = []
    for index, mask in enumerate(masks):
        wait = pair_sums if index else []
        sent = back_blocks(after(orders[mask + 1], *wait), wk, wv, flat, share)
        arrived.append(lax.ppermute(sent, "tgt", partners(n_tgt, 1)))
    parts, blocks = [], keys
    for mask, block in zip(masks, arrived):
        blocks = back_blocks(after(orders[mask], *blocks), wk, wv, flat, share, block)
        for side in reversed(range(n_mdl)):
            block = blocks[side]
            if mask or side:
                pairs = [
                    (a * n_mdl + b, (a ^ mask) * n_mdl + (b ^ side))
                    for a in range(n_tgt)
                    for b in range(n_mdl)
                ]
                block = lax.ppermute(block, ("tgt", "mdl"), pairs)
            parts.append(block)

    query_grads = None
    if line:
        pair_sums += [pair_sum(layer, *blocks) for layer in range(1, layers)]
        opposite = [(0, 3), (3, 0), (1, 2), (2, 1)]
        mine = [
            to_owners(plus(value, lax.ppermute(value, "inp", opposite), spread=True), n_tgt)
            for value in pair_sums
        ]
        other = [lax.ppermute(value, "inp", partners(n_inp, 1)) for value in mine]
    else:
        mine, other = ([to_owners(lax.psum(value, "inp"), n_tgt) for value in half] for half in (keep, send))
    for layer in range(layers):
        query_grads = join_heads(place, mine[layer], other[layer], layer, layers, query_grads)
    return query_grads, total_of(parts)


def solution(mesh):
    placed = (
        P("inp", None),
        P(None, None, "mdl", "tgt", None),
        P(None, None, "mdl", "tgt", None),
        P(None, "tgt", "mdl", None),
        P(None, "tgt", "mdl", None),
    )
    return jax.shard_map(
        body,
        mesh=mesh,
        in_specs=placed,
        out_specs=(P(None, "tgt", "mdl", None), P("inp", ("tgt", "mdl"))),
        check_vma=False,
    )
```

```python
import functools

import jax
import jax.numpy as jnp
from jax import lax
from jax.experimental import pallas as pl
from jax.experimental.pallas import tpu as pltpu
from jax.sharding import PartitionSpec as P

F32, BF16 = jnp.float32, jnp.bfloat16
MIB = 1024 * 1024
PARTS = 1
NT = (((1,), (1,)), ((), ()))
NN = (((1,), (0,)), ((), ()))
TN = (((0,), (0,)), ((), ()))


def dot(left, right, dims):
    return lax.dot_general(left, right, dims, preferred_element_type=F32)


def params():
    return pltpu.CompilerParams(vmem_limit_bytes=24 * MIB)


def cost(flops, nbytes, exps=0):
    return pl.CostEstimate(flops=int(flops), bytes_accessed=int(nbytes), transcendentals=int(exps))


def in_hbm(*arrays):
    return [pltpu.with_memory_space_constraint(array, pltpu.HBM) for array in arrays]


def partners(count, mask):
    return [(index, index ^ mask) for index in range(count)]


def pick_kernel(head_ref, *refs):
    count = sum(len(ref.shape) == 4 for ref in refs)
    sources, outs = refs[:count], refs[count:]
    for index, source in enumerate(sources):
        if len(outs) == count:
            outs[index][...] = source[0]
        else:
            layers = source.shape[1]
            outs[0][index * layers : (index + 1) * layers] = source[0]


def pick(head, parts, together=False):
    shape = parts[0][0].shape
    specs, sizes = [], []
    for source, first, count in parts:
        specs.append(
            pl.BlockSpec((1, count) + shape[2:], lambda i, head, first=first: (head[0], first, 0, 0))
        )
        sizes.append(count)
    sizes = [sum(sizes)] if together else sizes
    outs = [jax.ShapeDtypeStruct((size,) + shape[2:], BF16) for size in sizes]
    return pl.pallas_call(
        pick_kernel,
        grid_spec=pltpu.PrefetchScalarGridSpec(
            num_scalar_prefetch=1,
            grid=(1,),
            in_specs=specs,
            out_specs=[pl.BlockSpec(out.shape, lambda i, head: (0, 0, 0)) for out in outs],
        ),
        out_shape=outs,
        compiler_params=params(),
        cost_estimate=cost(0, 4 * sum(out.size for out in outs)),
    )(head, *[source for source, _, _ in parts])


def join_kernel(place_ref, part_ref, *rest):
    out = rest[-1]
    for head in range(part_ref.shape[0]):
        out[0, :, head, :] = part_ref[place_ref[0] ^ head]


def join_heads(place, part, mine, layer, layers, begun):
    heads, rows, size = part.shape
    extra = [] if begun is None else [begun]

    def half(i, place):
        return (layer, (1 - place[2]) if mine else place[2], 0, 0)

    return pl.pallas_call(
        join_kernel,
        grid_spec=pltpu.PrefetchScalarGridSpec(
            num_scalar_prefetch=1,
            grid=(1,),
            in_specs=[whole(part.shape)] + [pl.BlockSpec(memory_space=pl.ANY)] * len(extra),
            out_specs=pl.BlockSpec((1, rows, heads, size), half),
        ),
        out_shape=jax.ShapeDtypeStruct((layers, 2 * rows, heads, size), BF16),
        input_output_aliases={2: 0} if extra else {},
        compiler_params=params(),
        cost_estimate=cost(0, 4 * rows * heads * size),
    )(place, part, *extra)


def project_kernel(enc_ref, wk_ref, wv_ref, k_ref, v_ref, sums):
    step = pl.program_id(0)

    @pl.when(step == 0)
    def _():
        sums[...] = jnp.zeros_like(sums)

    sums[0] += dot(enc_ref[...], wk_ref[0], NN)
    sums[1] += dot(enc_ref[...], wv_ref[0], NN)

    @pl.when(step == pl.num_programs(0) - 1)
    def _():
        k_ref[0] = sums[0].astype(BF16)
        v_ref[0] = sums[1].astype(BF16)


def project(encoder, wk, wv, layer):
    rows, width = encoder.shape
    size = wk.shape[2]
    depth = width // 4
    weight = pl.BlockSpec((1, depth, size), lambda i: (layer, i, 0))
    result = whole((1, rows, size))
    return pl.pallas_call(
        project_kernel,
        grid=(width // depth,),
        in_specs=[pl.BlockSpec((rows, depth), lambda i: (0, i)), weight, weight],
        out_specs=[result, result],
        out_shape=[jax.ShapeDtypeStruct((1, rows, size), BF16)] * 2,
        scratch_shapes=[pltpu.VMEM((2, rows, size), F32)],
        compiler_params=params(),
        cost_estimate=cost(4 * rows * width * size, 2 * width * (rows + 2 * size)),
    )(*in_hbm(encoder, wk, wv))


def columns(index, count, rows, place_ref):
    if index < count - 2:
        return slice(index * rows, (index + 1) * rows)
    start = (count - 2 + ((index - count + 2) ^ place_ref[1])) * rows
    return pl.ds(pl.multiple_of(start, rows), rows)


def block_of(ref):
    return ref[(0,) * (len(ref.shape) - 2)]


def stats_kernel(place_ref, k_ref, v_ref, *refs):
    out, pieces = refs[-1], refs[:-1]
    count = len(pieces) // 2
    for index in range(count):
        query, cotangent = block_of(pieces[index]), block_of(pieces[count + index])
        cols = columns(index, count, query.shape[0], place_ref)
        scores = dot(block_of(k_ref), query, NT)
        peak = jnp.max(scores, axis=0, keepdims=True)
        shifted = jnp.exp(scores - peak)
        dprobs = dot(block_of(v_ref), cotangent, NT)
        out[0:1, cols] = peak
        out[1:2, cols] = jnp.sum(shifted, axis=0, keepdims=True)
        out[2:3, cols] = jnp.sum(shifted * dprobs, axis=0, keepdims=True)
        out[3:4, cols] = jnp.zeros_like(peak)


def whole(shape):
    return pl.BlockSpec(shape, lambda i, *place: (0,) * len(shape))


def block_at(array, index):
    if len(array.shape) == 4:
        return pl.BlockSpec((1, 1) + array.shape[2:], lambda i, place: (place[0], index, 0, 0))
    return pl.BlockSpec((1,) + array.shape[1:], lambda i, place: (index, 0, 0))


def row_stats(place, keys, values, pieces):
    enc_rows, size = keys.shape[1:]
    total = pieces[0][0].shape[-2] * len(pieces) // 2
    return pl.pallas_call(
        stats_kernel,
        grid_spec=pltpu.PrefetchScalarGridSpec(
            num_scalar_prefetch=1,
            grid=(1,),
            in_specs=[block_at(*piece) for piece in [(keys, 0), (values, 0), *pieces]],
            out_specs=whole((4, total)),
        ),
        out_shape=jax.ShapeDtypeStruct((4, total), F32),
        compiler_params=params(),
        cost_estimate=cost(
            4 * enc_rows * total * size, 4 * size * (enc_rows + total), enc_rows * total
        ),
    )(place, keys, values, *[array for array, _ in pieces])


def grads_kernel(count, place_ref, k_ref, v_ref, *refs):
    queries, cotangents, refs = refs[:count], refs[count : 2 * count], refs[2 * count :]
    stats, refs, (dk_ref, dv_ref) = refs[: -2 * PARTS - 2], refs[-2 * PARTS - 2 : -2], refs[-2:]
    keys, values = block_of(k_ref), block_of(v_ref)
    rows = refs[0].shape[1]
    for index in range(count):
        query, cotangent = block_of(queries[index]), block_of(cotangents[index])
        cols = columns(index, count, query.shape[0], place_ref)
        parts = [part[:, cols] for part in stats]
        peak = functools.reduce(jnp.maximum, [part[0:1] for part in parts])
        scales = [jnp.exp(part[0:1] - peak) for part in parts]
        total = sum(part[1:2] * scale for part, scale in zip(parts, scales))
        inner = sum(part[2:3] * scale for part, scale in zip(parts, scales)) / total
        attention = jnp.exp(dot(keys, query, NT) - peak) * (1.0 / total)
        dprobs = dot(values, cotangent, NT)
        dscores = (attention * (dprobs - inner)).astype(BF16)
        query_grad = dot(dscores, keys, TN).astype(BF16)
        slot = index if index < count - 2 else count - 2 + ((index - count + 2) ^ place_ref[1])
        first = place_ref[2] != 0
        for part in range(PARTS):
            upper = query_grad[part * rows : (part + 1) * rows]
            lower = query_grad[(PARTS + part) * rows : (PARTS + part + 1) * rows]
            refs[part][slot] = jnp.where(first, upper, lower)
            refs[PARTS + part][slot] = jnp.where(first, lower, upper)
        key_part = dot(dscores, query, NN)
        value_part = dot(attention.astype(BF16), cotangent, NN)
        key_sum = key_part if index == 0 else key_sum + key_part
        value_sum = value_part if index == 0 else value_sum + value_part
    dk_ref[...] = key_sum.astype(BF16)
    dv_ref[...] = value_sum.astype(BF16)


def attention_grads(place, keys, values, pieces, stats):
    enc_rows, size = keys.shape[1:]
    rows = pieces[0][0].shape[-2]
    count = len(pieces) // 2
    total = rows * count
    outs = [(count, rows // (2 * PARTS), size)] * (2 * PARTS) + [(enc_rows, size)] * 2
    return pl.pallas_call(
        functools.partial(grads_kernel, count),
        grid_spec=pltpu.PrefetchScalarGridSpec(
            num_scalar_prefetch=1,
            grid=(1,),
            in_specs=[block_at(*piece) for piece in [(keys, 0), (values, 0), *pieces]]
            + [whole((4, total))] * len(stats),
            out_specs=[whole(shape) for shape in outs],
        ),
        out_shape=[jax.ShapeDtypeStruct(shape, BF16) for shape in outs],
        compiler_params=params(),
        cost_estimate=cost(
            10 * enc_rows * total * size, 6 * size * (enc_rows + total), enc_rows * total
        ),
    )(place, keys, values, *[array for array, _ in pieces], *stats)


def back_kernel(order_ref, wk_ref, wv_ref, *refs):
    flat, out = refs[:-1], refs[-1]
    total = None
    for layer in range(wk_ref.shape[0]):
        part = dot(flat[2 * layer][...], wk_ref[layer], NT) + dot(flat[2 * layer + 1][...], wv_ref[layer], NT)
        total = part if total is None else total + part
    out[0] = total.astype(out.dtype)


def back_blocks(order, wk, wv, flat, share, dtype):
    layers, _, size = wk.shape
    rows = flat[0].shape[0]
    blocks = order.shape[0]
    weight = pl.BlockSpec((layers, share, size), lambda i, order: (0, order[i], 0))
    return pl.pallas_call(
        back_kernel,
        grid_spec=pltpu.PrefetchScalarGridSpec(
            num_scalar_prefetch=1,
            grid=(blocks,),
            in_specs=[weight, weight] + [pl.BlockSpec((rows, size), lambda i, order: (0, 0))] * len(flat),
            out_specs=pl.BlockSpec((1, rows, share), lambda i, order: (i, 0, 0)),
        ),
        out_shape=jax.ShapeDtypeStruct((blocks, rows, share), dtype),
        compiler_params=params(),
        cost_estimate=cost(
            4 * layers * rows * size * share * blocks, 2 * blocks * share * (2 * layers * size + 2 * rows)
        ),
    )(order, *in_hbm(wk, wv), *flat)


def plus_kernel(one_ref, two_ref, *outs):
    total = (one_ref[...].astype(F32) + two_ref[...].astype(F32)).astype(BF16)
    for index, out in enumerate(outs):
        out[...] = total if len(outs) == 1 else total[index]


def plus(one, two, spread=False):
    shape = one.shape[1:] if spread else one.shape
    outs = [jax.ShapeDtypeStruct(shape, BF16)] * (one.shape[0] if spread else 1)
    results = pl.pallas_call(
        plus_kernel,
        grid=(1,),
        in_specs=[whole(one.shape)] * 2,
        out_specs=[whole(shape)] * len(outs),
        out_shape=outs,
        compiler_params=params(),
        cost_estimate=cost(one.size, 6 * one.size),
    )(one, two)
    return results if spread else results[0]


def stack_kernel(*refs):
    for index, ref in enumerate(refs[:-1]):
        refs[-1][index] = ref[...]


def stacked(parts):
    shape = (len(parts),) + parts[0].shape
    return pl.pallas_call(
        stack_kernel,
        grid=(1,),
        in_specs=[whole(parts[0].shape)] * len(parts),
        out_specs=whole(shape),
        out_shape=jax.ShapeDtypeStruct(shape, BF16),
        compiler_params=params(),
        cost_estimate=cost(0, 4 * len(parts) * parts[0].size),
    )(*parts)


def total_kernel(*refs):
    total = refs[0][0].astype(F32)
    for ref in refs[1:-1]:
        total = total + ref[0].astype(F32)
    refs[-1][0] = total.astype(BF16)


def total_of(parts):
    shape = (1,) + parts[0][0].shape[1:]
    return pl.pallas_call(
        total_kernel,
        grid=(1,),
        in_specs=[pl.BlockSpec(shape, lambda i, index=index: (index, 0, 0)) for _, index in parts],
        out_specs=whole(shape),
        out_shape=jax.ShapeDtypeStruct(shape, BF16),
        compiler_params=params(),
        cost_estimate=cost(0, 0),
    )(*[array for array, _ in parts])


def exchange(value, n_inp, n_tgt, mask_of):
    pairs = [(z * n_tgt + t, z * n_tgt + (t ^ mask_of(z))) for z in range(n_inp) for t in range(n_tgt)]
    return lax.ppermute(value, ("inp", "tgt"), pairs)


def everywhere(value, n_inp):
    return [value] + [
        lax.ppermute(value, "inp", [(i, (i + shift) % n_inp) for i in range(n_inp)])
        for shift in range(1, n_inp)
    ]


def after(value, *others):
    return lax.optimization_barrier((value, *others))[0]


def to_owners(parts, n_tgt):
    return stacked(
        [part if mask == 0 else lax.ppermute(part, "tgt", partners(n_tgt, mask)) for mask, part in enumerate(parts)]
    )


def body(encoder, key_weight, value_weight, queries, grad_out):
    layers, dec_rows, heads, size = queries.shape
    width = encoder.shape[1]
    n_inp, n_tgt, n_mdl = (lax.axis_size(axis) for axis in ("inp", "tgt", "mdl"))
    z, t, m = (lax.axis_index(axis) for axis in ("inp", "tgt", "mdl"))
    share = width // (n_tgt * n_mdl)
    wk = key_weight.reshape(layers, width, size)
    wv = value_weight.reshape(layers, width, size)
    line = n_inp == 4
    odd = (z % 2).astype(jnp.int32)
    upper = ((z == 0) | (z == n_inp - 1)).astype(jnp.int32) if line else jnp.ones_like(odd)
    place = jnp.stack([t.astype(jnp.int32), odd, upper])
    wanted_head, beside_head = (t ^ (2 + odd))[None], (t ^ 1)[None]
    orders = [
        jnp.stack([(t ^ mask) * n_mdl + (m ^ side) for mask in masks for side in range(n_mdl)]).astype(jnp.int32)
        for masks in ((3, 1), (2, 0))
    ]
    queries, place, wanted_head, beside_head, *orders = lax.optimization_barrier(
        (queries, place, wanted_head, beside_head, *orders)
    )

    own = [jnp.transpose(array, (2, 0, 1, 3)) for array in (queries, grad_out)]
    wanted = []
    for layer in range(layers):
        first = after(wanted_head, *wanted)
        wanted += pick(first, [(source, layer, 1) for source in own], together=True)
    fetched = [exchange(piece, n_inp, n_tgt, lambda z: 2 + z % 2) for piece in wanted]
    keys, values, begun = [], [], wanted
    for layer in range(layers):
        key_block, value_block = project(after(encoder, *begun), wk, wv, layer)
        begun = fetched[:1]
        keys.append(key_block)
        values.append(value_block)
    (beside,) = pick(after(beside_head, keys[0]), [(source, 0, layers) for source in own], together=True)
    beside = lax.ppermute(beside, "tgt", partners(n_tgt, 1))
    handed = [
        lax.ppermute(after(piece, key_block), "inp", partners(n_inp, 1)) for piece, key_block in zip(fetched, keys)
    ]

    pieces, stats = [], []
    for layer in range(layers):
        pieces.append(
            [
                piece
                for kind in range(2)
                for piece in (
                    (own[kind], layer),
                    (beside, kind * layers + layer),
                    (fetched[layer], kind),
                    (handed[layer], kind),
                )
            ]
        )
        own_stats = row_stats(after(place, *[part[0] for part in stats]), keys[layer], values[layer], pieces[layer])
        stats.append(everywhere(own_stats, n_inp))
    flat, keep, send = [], [], []
    pair_sums, totals, mine, other = [], [], [], []

    def pair_sum(*others):
        index = len(pair_sums)
        if not line:
            pair_sums.append(keep[index])
        else:
            arrived = lax.ppermute(send[index], "inp", partners(n_inp, 1))
            pair_sums.append(plus(after(keep[index], *others), arrived))
        return pair_sums[-1]

    def line_sum(*others):
        index = len(totals)
        if not line:
            totals.append([lax.psum(keep[index], "inp")[mask] for mask in range(n_tgt)])
            mine.append(to_owners(totals[-1], n_tgt))
            other.append(to_owners([lax.psum(send[index], "inp")[mask] for mask in range(n_tgt)], n_tgt))
        else:
            value = pair_sums[index]
            earlier = [part for total in totals[-1:] for part in total]
            arrived = lax.ppermute(after(value, *earlier), "inp", [(0, 3), (3, 0), (1, 2), (2, 1)])
            totals.append(plus(after(value, *others), arrived, spread=True))
            mine.append(to_owners(totals[-1], n_tgt))
            other.append(lax.ppermute(mine[-1], "inp", partners(n_inp, 1)))
        return totals[-1]

    for layer in range(layers):
        results = attention_grads(after(place, *flat), keys[layer], values[layer], pieces[layer], stats[layer])
        keep += results[:PARTS]
        send += results[PARTS : 2 * PARTS]
        flat += results[2 * PARTS :]
    send[0] = after(send[0], *stats[-1])
    chunks = len(keep)

    sent = back_blocks(orders[0], wk, wv, flat, share, BF16)
    pair_sum(sent)
    while len(pair_sums) < chunks:
        send[len(pair_sums)] = after(send[len(pair_sums)], pair_sums[-1])
        pair_sum()
    arrived = lax.ppermute(after(sent, pair_sums[0]), "tgt", partners(n_tgt, 1))
    own_blocks = back_blocks(after(orders[1], pair_sums[0]), wk, wv, flat, share, F32)
    arrived = after(arrived, pair_sums[0])
    far_own, far_other = (total_of([(own_blocks, side), (arrived, side)]) for side in range(2))
    waits = [far_own, far_other]
    far_other = lax.ppermute(far_other, "tgt", partners(n_tgt, 2))
    far_own = lax.ppermute(far_own, "tgt", partners(n_tgt, 2))
    line_sum(*waits)
    side_own = total_of([(own_blocks, 3), (arrived, 3), (far_other, 0)])
    side_own = lax.ppermute(side_own, "mdl", partners(n_mdl, 1))
    while len(totals) < chunks:
        line_sum(side_own, far_own, mine[0])
    query_grads = None
    for layer in range(layers):
        query_grads = join_heads(place, mine[layer], True, layer, layers, query_grads)
        query_grads = join_heads(place, other[layer], False, layer, layers, query_grads)
    enc_grad = total_of([(own_blocks, 2), (arrived, 2), (far_own, 0), (side_own, 0)])
    return query_grads, enc_grad[0]


def solution(mesh):
    placed = (
        P("inp", None),
        P(None, None, "mdl", "tgt", None),
        P(None, None, "mdl", "tgt", None),
        P(None, "tgt", "mdl", None),
        P(None, "tgt", "mdl", None),
    )
    return jax.shard_map(
        body,
        mesh=mesh,
        in_specs=placed,
        out_specs=(P(None, "tgt", "mdl", None), P("inp", ("tgt", "mdl"))),
        check_vma=False,
    )
```

```python
import functools

import jax
import jax.numpy as jnp
from jax import lax
from jax.experimental import pallas as pl
from jax.experimental.pallas import tpu as pltpu
from jax.sharding import PartitionSpec as P

F32, BF16 = jnp.float32, jnp.bfloat16
MIB = 1024 * 1024
PARTS = 1
NT = (((1,), (1,)), ((), ()))
NN = (((1,), (0,)), ((), ()))
TN = (((0,), (0,)), ((), ()))


def dot(left, right, dims):
    return lax.dot_general(left, right, dims, preferred_element_type=F32)


def params():
    return pltpu.CompilerParams(vmem_limit_bytes=24 * MIB)


def cost(flops, nbytes, exps=0):
    return pl.CostEstimate(flops=int(flops), bytes_accessed=int(nbytes), transcendentals=int(exps))


def in_hbm(*arrays):
    return [pltpu.with_memory_space_constraint(array, pltpu.HBM) for array in arrays]


def partners(count, mask):
    return [(index, index ^ mask) for index in range(count)]


def pick_kernel(head_ref, *refs):
    count = sum(len(ref.shape) == 4 for ref in refs)
    sources, outs = refs[:count], refs[count:]
    for index, source in enumerate(sources):
        if len(outs) == count:
            outs[index][...] = source[0]
        else:
            layers = source.shape[1]
            outs[0][index * layers : (index + 1) * layers] = source[0]


def pick(head, parts, together=False):
    shape = parts[0][0].shape
    specs, sizes = [], []
    for source, first, count in parts:
        specs.append(
            pl.BlockSpec((1, count) + shape[2:], lambda i, head, first=first: (head[0], first, 0, 0))
        )
        sizes.append(count)
    sizes = [sum(sizes)] if together else sizes
    outs = [jax.ShapeDtypeStruct((size,) + shape[2:], BF16) for size in sizes]
    return pl.pallas_call(
        pick_kernel,
        grid_spec=pltpu.PrefetchScalarGridSpec(
            num_scalar_prefetch=1,
            grid=(1,),
            in_specs=specs,
            out_specs=[pl.BlockSpec(out.shape, lambda i, head: (0, 0, 0)) for out in outs],
        ),
        out_shape=outs,
        compiler_params=params(),
        cost_estimate=cost(0, 4 * sum(out.size for out in outs)),
    )(head, *[source for source, _, _ in parts])


def join_kernel(place_ref, part_ref, *rest):
    out = rest[-1]
    for head in range(part_ref.shape[0]):
        out[0, :, head, :] = part_ref[place_ref[0] ^ head]


def join_heads(place, part, mine, layer, layers, begun):
    heads, rows, size = part.shape
    extra = [] if begun is None else [begun]

    def half(i, place):
        return (layer, (1 - place[2]) if mine else place[2], 0, 0)

    return pl.pallas_call(
        join_kernel,
        grid_spec=pltpu.PrefetchScalarGridSpec(
            num_scalar_prefetch=1,
            grid=(1,),
            in_specs=[whole(part.shape)] + [pl.BlockSpec(memory_space=pl.ANY)] * len(extra),
            out_specs=pl.BlockSpec((1, rows, heads, size), half),
        ),
        out_shape=jax.ShapeDtypeStruct((layers, 2 * rows, heads, size), BF16),
        input_output_aliases={2: 0} if extra else {},
        compiler_params=params(),
        cost_estimate=cost(0, 4 * rows * heads * size),
    )(place, part, *extra)


def project_kernel(enc_ref, wk_ref, wv_ref, k_ref, v_ref, sums):
    step = pl.program_id(0)

    @pl.when(step == 0)
    def _():
        sums[...] = jnp.zeros_like(sums)

    sums[0] += dot(enc_ref[...], wk_ref[0], NN)
    sums[1] += dot(enc_ref[...], wv_ref[0], NN)

    @pl.when(step == pl.num_programs(0) - 1)
    def _():
        k_ref[0] = sums[0].astype(BF16)
        v_ref[0] = sums[1].astype(BF16)


def project(encoder, wk, wv, layer):
    rows, width = encoder.shape
    size = wk.shape[2]
    depth = width // 4
    weight = pl.BlockSpec((1, depth, size), lambda i: (layer, i, 0))
    result = whole((1, rows, size))
    return pl.pallas_call(
        project_kernel,
        grid=(width // depth,),
        in_specs=[pl.BlockSpec((rows, depth), lambda i: (0, i)), weight, weight],
        out_specs=[result, result],
        out_shape=[jax.ShapeDtypeStruct((1, rows, size), BF16)] * 2,
        scratch_shapes=[pltpu.VMEM((2, rows, size), F32)],
        compiler_params=params(),
        cost_estimate=cost(4 * rows * width * size, 2 * width * (rows + 2 * size)),
    )(*in_hbm(encoder, wk, wv))


def columns(index, count, rows, place_ref):
    if index < count - 2:
        return slice(index * rows, (index + 1) * rows)
    start = (count - 2 + ((index - count + 2) ^ place_ref[1])) * rows
    return pl.ds(pl.multiple_of(start, rows), rows)


def block_of(ref):
    return ref[(0,) * (len(ref.shape) - 2)]


def stats_kernel(place_ref, k_ref, v_ref, *refs):
    out, pieces = refs[-1], refs[:-1]
    count = len(pieces) // 2
    for index in range(count):
        query, cotangent = block_of(pieces[index]), block_of(pieces[count + index])
        cols = columns(index, count, query.shape[0], place_ref)
        scores = dot(block_of(k_ref), query, NT)
        peak = jnp.max(scores, axis=0, keepdims=True)
        shifted = jnp.exp(scores - peak)
        dprobs = dot(block_of(v_ref), cotangent, NT)
        out[0:1, cols] = peak
        out[1:2, cols] = jnp.sum(shifted, axis=0, keepdims=True)
        out[2:3, cols] = jnp.sum(shifted * dprobs, axis=0, keepdims=True)
        out[3:4, cols] = jnp.zeros_like(peak)


def whole(shape):
    return pl.BlockSpec(shape, lambda i, *place: (0,) * len(shape))


def block_at(array, index):
    if len(array.shape) == 4:
        return pl.BlockSpec((1, 1) + array.shape[2:], lambda i, place: (place[0], index, 0, 0))
    return pl.BlockSpec((1,) + array.shape[1:], lambda i, place: (index, 0, 0))


def row_stats(place, keys, values, pieces):
    enc_rows, size = keys.shape[1:]
    total = pieces[0][0].shape[-2] * len(pieces) // 2
    return pl.pallas_call(
        stats_kernel,
        grid_spec=pltpu.PrefetchScalarGridSpec(
            num_scalar_prefetch=1,
            grid=(1,),
            in_specs=[block_at(*piece) for piece in [(keys, 0), (values, 0), *pieces]],
            out_specs=whole((4, total)),
        ),
        out_shape=jax.ShapeDtypeStruct((4, total), F32),
        compiler_params=params(),
        cost_estimate=cost(
            4 * enc_rows * total * size, 4 * size * (enc_rows + total), enc_rows * total
        ),
    )(place, keys, values, *[array for array, _ in pieces])


def grads_kernel(count, place_ref, k_ref, v_ref, *refs):
    queries, cotangents, refs = refs[:count], refs[count : 2 * count], refs[2 * count :]
    stats, refs, (dk_ref, dv_ref) = refs[: -2 * PARTS - 2], refs[-2 * PARTS - 2 : -2], refs[-2:]
    keys, values = block_of(k_ref), block_of(v_ref)
    rows = refs[0].shape[1]
    for index in range(count):
        query, cotangent = block_of(queries[index]), block_of(cotangents[index])
        cols = columns(index, count, query.shape[0], place_ref)
        parts = [part[:, cols] for part in stats]
        peak = functools.reduce(jnp.maximum, [part[0:1] for part in parts])
        scales = [jnp.exp(part[0:1] - peak) for part in parts]
        total = sum(part[1:2] * scale for part, scale in zip(parts, scales))
        inner = sum(part[2:3] * scale for part, scale in zip(parts, scales)) / total
        attention = jnp.exp(dot(keys, query, NT) - peak) * (1.0 / total)
        dprobs = dot(values, cotangent, NT)
        dscores = (attention * (dprobs - inner)).astype(BF16)
        query_grad = dot(dscores, keys, TN).astype(BF16)
        slot = index if index < count - 2 else count - 2 + ((index - count + 2) ^ place_ref[1])
        first = place_ref[2] != 0
        for part in range(PARTS):
            upper = query_grad[part * rows : (part + 1) * rows]
            lower = query_grad[(PARTS + part) * rows : (PARTS + part + 1) * rows]
            refs[part][slot] = jnp.where(first, upper, lower)
            refs[PARTS + part][slot] = jnp.where(first, lower, upper)
        key_part = dot(dscores, query, NN)
        value_part = dot(attention.astype(BF16), cotangent, NN)
        key_sum = key_part if index == 0 else key_sum + key_part
        value_sum = value_part if index == 0 else value_sum + value_part
    dk_ref[...] = key_sum.astype(BF16)
    dv_ref[...] = value_sum.astype(BF16)


def attention_grads(place, keys, values, pieces, stats):
    enc_rows, size = keys.shape[1:]
    rows = pieces[0][0].shape[-2]
    count = len(pieces) // 2
    total = rows * count
    outs = [(count, rows // (2 * PARTS), size)] * (2 * PARTS) + [(enc_rows, size)] * 2
    return pl.pallas_call(
        functools.partial(grads_kernel, count),
        grid_spec=pltpu.PrefetchScalarGridSpec(
            num_scalar_prefetch=1,
            grid=(1,),
            in_specs=[block_at(*piece) for piece in [(keys, 0), (values, 0), *pieces]]
            + [whole((4, total))] * len(stats),
            out_specs=[whole(shape) for shape in outs],
        ),
        out_shape=[jax.ShapeDtypeStruct(shape, BF16) for shape in outs],
        compiler_params=params(),
        cost_estimate=cost(
            10 * enc_rows * total * size, 6 * size * (enc_rows + total), enc_rows * total
        ),
    )(place, keys, values, *[array for array, _ in pieces], *stats)


def back_kernel(order_ref, wk_ref, wv_ref, *refs):
    flat, out = refs[:-1], refs[-1]
    total = None
    for layer in range(wk_ref.shape[0]):
        part = dot(flat[2 * layer][...], wk_ref[layer], NT) + dot(flat[2 * layer + 1][...], wv_ref[layer], NT)
        total = part if total is None else total + part
    out[0] = total.astype(out.dtype)


def back_blocks(order, wk, wv, flat, share, dtype):
    layers, _, size = wk.shape
    rows = flat[0].shape[0]
    blocks = order.shape[0]
    weight = pl.BlockSpec((layers, share, size), lambda i, order: (0, order[i], 0))
    return pl.pallas_call(
        back_kernel,
        grid_spec=pltpu.PrefetchScalarGridSpec(
            num_scalar_prefetch=1,
            grid=(blocks,),
            in_specs=[weight, weight] + [pl.BlockSpec((rows, size), lambda i, order: (0, 0))] * len(flat),
            out_specs=pl.BlockSpec((1, rows, share), lambda i, order: (i, 0, 0)),
        ),
        out_shape=jax.ShapeDtypeStruct((blocks, rows, share), dtype),
        compiler_params=params(),
        cost_estimate=cost(
            4 * layers * rows * size * share * blocks, 2 * blocks * share * (2 * layers * size + 2 * rows)
        ),
    )(order, *in_hbm(wk, wv), *flat)


def plus_kernel(one_ref, two_ref, *outs):
    total = (one_ref[...].astype(F32) + two_ref[...].astype(F32)).astype(BF16)
    for index, out in enumerate(outs):
        out[...] = total if len(outs) == 1 else total[index]


def plus(one, two, spread=False):
    shape = one.shape[1:] if spread else one.shape
    outs = [jax.ShapeDtypeStruct(shape, BF16)] * (one.shape[0] if spread else 1)
    results = pl.pallas_call(
        plus_kernel,
        grid=(1,),
        in_specs=[whole(one.shape)] * 2,
        out_specs=[whole(shape)] * len(outs),
        out_shape=outs,
        compiler_params=params(),
        cost_estimate=cost(one.size, 6 * one.size),
    )(one, two)
    return results if spread else results[0]


def stack_kernel(*refs):
    for index, ref in enumerate(refs[:-1]):
        refs[-1][index] = ref[...]


def stacked(parts):
    shape = (len(parts),) + parts[0].shape
    return pl.pallas_call(
        stack_kernel,
        grid=(1,),
        in_specs=[whole(parts[0].shape)] * len(parts),
        out_specs=whole(shape),
        out_shape=jax.ShapeDtypeStruct(shape, BF16),
        compiler_params=params(),
        cost_estimate=cost(0, 4 * len(parts) * parts[0].size),
    )(*parts)


def total_kernel(*refs):
    total = refs[0][0].astype(F32)
    for ref in refs[1:-1]:
        total = total + ref[0].astype(F32)
    refs[-1][0] = total.astype(BF16)


def total_of(parts):
    shape = (1,) + parts[0][0].shape[1:]
    return pl.pallas_call(
        total_kernel,
        grid=(1,),
        in_specs=[pl.BlockSpec(shape, lambda i, index=index: (index, 0, 0)) for _, index in parts],
        out_specs=whole(shape),
        out_shape=jax.ShapeDtypeStruct(shape, BF16),
        compiler_params=params(),
        cost_estimate=cost(0, 0),
    )(*[array for array, _ in parts])


def exchange(value, n_inp, n_tgt, mask_of):
    pairs = [(z * n_tgt + t, z * n_tgt + (t ^ mask_of(z))) for z in range(n_inp) for t in range(n_tgt)]
    return lax.ppermute(value, ("inp", "tgt"), pairs)


def everywhere(value, n_inp):
    return [value] + [
        lax.ppermute(value, "inp", partners(n_inp, mask)) for mask in range(1, n_inp)
    ]


def after(value, *others):
    return lax.optimization_barrier((value, *others))[0]


def to_owners(parts, n_tgt):
    return stacked(
        [part if mask == 0 else lax.ppermute(part, "tgt", partners(n_tgt, mask)) for mask, part in enumerate(parts)]
    )


def body(encoder, key_weight, value_weight, queries, grad_out):
    layers, dec_rows, heads, size = queries.shape
    width = encoder.shape[1]
    n_inp, n_tgt, n_mdl = (lax.axis_size(axis) for axis in ("inp", "tgt", "mdl"))
    z, t, m = (lax.axis_index(axis) for axis in ("inp", "tgt", "mdl"))
    share = width // (n_tgt * n_mdl)
    wk = key_weight.reshape(layers, width, size)
    wv = value_weight.reshape(layers, width, size)
    line = n_inp == 4
    odd = (z % 2).astype(jnp.int32)
    upper = ((z == 0) | (z == n_inp - 1)).astype(jnp.int32) if line else jnp.ones_like(odd)
    place = jnp.stack([t.astype(jnp.int32), odd, upper])
    plain = jnp.stack([t.astype(jnp.int32), jnp.zeros_like(odd), upper])
    wanted_head, beside_head, heads_along = (t ^ (2 + odd))[None], (t ^ 1)[None], [(t ^ 2)[None], (t ^ 3)[None]]
    orders = [
        jnp.stack([(t ^ mask) * n_mdl + (m ^ side) for mask in masks for side in range(n_mdl)]).astype(jnp.int32)
        for masks in ((3, 1), (2, 0))
    ]
    queries, place, plain, wanted_head, beside_head, heads_along, *orders = lax.optimization_barrier(
        (queries, place, plain, wanted_head, beside_head, heads_along, *orders)
    )
    places = [place] + [plain] * (layers - 1)

    own = [jnp.transpose(array, (2, 0, 1, 3)) for array in (queries, grad_out)]
    wanted = pick(wanted_head, [(source, 0, 1) for source in own], together=True)
    fetched = [exchange(wanted[0], n_inp, n_tgt, lambda z: 2 + z % 2)]
    for layer in range(1, layers):
        fetched.append([])
        for mask, head in zip((2, 3), heads_along):
            wanted += pick(after(head, *wanted), [(source, layer, 1) for source in own], together=True)
            fetched[layer].append(lax.ppermute(wanted[-1], "tgt", partners(n_tgt, mask)))
    keys, values, begun = [], [], wanted
    for layer in range(layers):
        key_block, value_block = project(after(encoder, *begun), wk, wv, layer)
        begun = fetched[:1]
        keys.append(key_block)
        values.append(value_block)
    (beside,) = pick(after(beside_head, keys[0]), [(source, 0, layers) for source in own], together=True)
    beside = lax.ppermute(beside, "tgt", partners(n_tgt, 1))
    handed = lax.ppermute(after(fetched[0], keys[0]), "inp", partners(n_inp, 1))
    along = [[fetched[0], handed]] + fetched[1:]

    pieces, stats = [], []
    for layer in range(layers):
        pieces.append(
            [
                piece
                for kind in range(2)
                for piece in (
                    (own[kind], layer),
                    (beside, kind * layers + layer),
                    (along[layer][0], kind),
                    (along[layer][1], kind),
                )
            ]
        )
    flat, keep, send = [], [], []
    pair_sums, totals, mine, other = [], [], [], []

    def pair_sum(*others):
        index = len(pair_sums)
        if not line:
            pair_sums.append(keep[index])
        else:
            arrived = lax.ppermute(send[index], "inp", partners(n_inp, 1))
            pair_sums.append(plus(after(keep[index], *others), arrived))
        return pair_sums[-1]

    def line_sum(*others):
        index = len(totals)
        if not line:
            totals.append([lax.psum(keep[index], "inp")[mask] for mask in range(n_tgt)])
            mine.append(to_owners(totals[-1], n_tgt))
            other.append(to_owners([lax.psum(send[index], "inp")[mask] for mask in range(n_tgt)], n_tgt))
        else:
            value = pair_sums[index]
            earlier = [part for total in totals[-1:] for part in total]
            arrived = lax.ppermute(after(value, *earlier), "inp", [(0, 3), (3, 0), (1, 2), (2, 1)])
            totals.append(plus(after(value, *others), arrived, spread=True))
            mine.append(to_owners(totals[-1], n_tgt))
            other.append(lax.ppermute(mine[-1], "inp", partners(n_inp, 1)))
        return totals[-1]

    for layer in range(layers):
        ready = flat if layer else [keys[1], along[1][0]]
        own_stats = row_stats(after(places[layer], *ready), keys[layer], values[layer], pieces[layer])
        stats.append(everywhere(own_stats, n_inp))
        results = attention_grads(
            after(places[layer], *flat), keys[layer], values[layer], pieces[layer], stats[layer]
        )
        keep += results[:PARTS]
        send += results[PARTS : 2 * PARTS]
        flat += results[2 * PARTS :]
    send[0] = after(send[0], *stats[-1])
    chunks = len(keep)

    sent = back_blocks(orders[0], wk, wv, flat, share, BF16)
    pair_sum(sent)
    while len(pair_sums) < chunks:
        send[len(pair_sums)] = after(send[len(pair_sums)], pair_sums[-1])
        pair_sum()
    arrived = lax.ppermute(after(sent, pair_sums[0]), "tgt", partners(n_tgt, 1))
    own_blocks = back_blocks(after(orders[1], pair_sums[0]), wk, wv, flat, share, F32)
    arrived = after(arrived, pair_sums[0])
    far_own, far_other = (total_of([(own_blocks, side), (arrived, side)]) for side in range(2))
    waits = [far_own, far_other]
    far_other = lax.ppermute(far_other, "tgt", partners(n_tgt, 2))
    far_own = lax.ppermute(far_own, "tgt", partners(n_tgt, 2))
    line_sum(*waits)
    side_own = total_of([(own_blocks, 3), (arrived, 3), (far_other, 0)])
    side_own = lax.ppermute(side_own, "mdl", partners(n_mdl, 1))
    while len(totals) < chunks:
        line_sum(side_own, far_own, mine[0])
    query_grads = None
    for layer in range(layers):
        query_grads = join_heads(place, mine[layer], True, layer, layers, query_grads)
        query_grads = join_heads(place, other[layer], False, layer, layers, query_grads)
    enc_grad = total_of([(own_blocks, 2), (arrived, 2), (far_own, 0), (side_own, 0)])
    return query_grads, enc_grad[0]


def solution(mesh):
    placed = (
        P("inp", None),
        P(None, None, "mdl", "tgt", None),
        P(None, None, "mdl", "tgt", None),
        P(None, "tgt", "mdl", None),
        P(None, "tgt", "mdl", None),
    )
    return jax.shard_map(
        body,
        mesh=mesh,
        in_specs=placed,
        out_specs=(P(None, "tgt", "mdl", None), P("inp", ("tgt", "mdl"))),
        check_vma=False,
    )
```

```python
import functools

import jax
import jax.numpy as jnp
from jax import lax
from jax.experimental import pallas as pl
from jax.experimental.pallas import tpu as pltpu
from jax.sharding import PartitionSpec as P

F32, BF16 = jnp.float32, jnp.bfloat16
MIB = 1024 * 1024
PARTS = 1
NT = (((1,), (1,)), ((), ()))
NN = (((1,), (0,)), ((), ()))
TN = (((0,), (0,)), ((), ()))


def dot(left, right, dims):
    return lax.dot_general(left, right, dims, preferred_element_type=F32)


def params():
    return pltpu.CompilerParams(vmem_limit_bytes=24 * MIB)


def cost(flops, nbytes, exps=0):
    return pl.CostEstimate(flops=int(flops), bytes_accessed=int(nbytes), transcendentals=int(exps))


def in_hbm(*arrays):
    return [pltpu.with_memory_space_constraint(array, pltpu.HBM) for array in arrays]


def partners(count, mask):
    return [(index, index ^ mask) for index in range(count)]


def pick_kernel(head_ref, *refs):
    count = sum(len(ref.shape) == 4 for ref in refs)
    sources, outs = refs[:count], refs[count:]
    for index, source in enumerate(sources):
        if len(outs) == count:
            outs[index][...] = source[0]
        else:
            layers = source.shape[1]
            outs[0][index * layers : (index + 1) * layers] = source[0]


def pick(head, parts, together=False):
    shape = parts[0][0].shape
    specs, sizes = [], []
    for source, first, count in parts:
        specs.append(
            pl.BlockSpec((1, count) + shape[2:], lambda i, head, first=first: (head[0], first, 0, 0))
        )
        sizes.append(count)
    sizes = [sum(sizes)] if together else sizes
    outs = [jax.ShapeDtypeStruct((size,) + shape[2:], BF16) for size in sizes]
    return pl.pallas_call(
        pick_kernel,
        grid_spec=pltpu.PrefetchScalarGridSpec(
            num_scalar_prefetch=1,
            grid=(1,),
            in_specs=specs,
            out_specs=[pl.BlockSpec(out.shape, lambda i, head: (0, 0, 0)) for out in outs],
        ),
        out_shape=outs,
        compiler_params=params(),
        cost_estimate=cost(0, 4 * sum(out.size for out in outs)),
    )(head, *[source for source, _, _ in parts])


def join_kernel(place_ref, part_ref, *rest):
    out = rest[-1]
    for head in range(part_ref.shape[0]):
        out[0, :, head, :] = part_ref[place_ref[0] ^ head]


def join_heads(place, part, mine, layer, layers, begun):
    heads, rows, size = part.shape
    extra = [] if begun is None else [begun]

    def half(i, place):
        return (layer, (1 - place[2]) if mine else place[2], 0, 0)

    return pl.pallas_call(
        join_kernel,
        grid_spec=pltpu.PrefetchScalarGridSpec(
            num_scalar_prefetch=1,
            grid=(1,),
            in_specs=[whole(part.shape)] + [pl.BlockSpec(memory_space=pl.ANY)] * len(extra),
            out_specs=pl.BlockSpec((1, rows, heads, size), half),
        ),
        out_shape=jax.ShapeDtypeStruct((layers, 2 * rows, heads, size), BF16),
        input_output_aliases={2: 0} if extra else {},
        compiler_params=params(),
        cost_estimate=cost(0, 4 * rows * heads * size),
    )(place, part, *extra)


def project_kernel(enc_ref, wk_ref, wv_ref, k_ref, v_ref, sums):
    step = pl.program_id(0)

    @pl.when(step == 0)
    def _():
        sums[...] = jnp.zeros_like(sums)

    sums[0] += dot(enc_ref[...], wk_ref[0], NN)
    sums[1] += dot(enc_ref[...], wv_ref[0], NN)

    @pl.when(step == pl.num_programs(0) - 1)
    def _():
        k_ref[0] = sums[0].astype(BF16)
        v_ref[0] = sums[1].astype(BF16)


def project(encoder, wk, wv, layer):
    rows, width = encoder.shape
    size = wk.shape[2]
    depth = width // 4
    weight = pl.BlockSpec((1, depth, size), lambda i: (layer, i, 0))
    result = whole((1, rows, size))
    return pl.pallas_call(
        project_kernel,
        grid=(width // depth,),
        in_specs=[pl.BlockSpec((rows, depth), lambda i: (0, i)), weight, weight],
        out_specs=[result, result],
        out_shape=[jax.ShapeDtypeStruct((1, rows, size), BF16)] * 2,
        scratch_shapes=[pltpu.VMEM((2, rows, size), F32)],
        compiler_params=params(),
        cost_estimate=cost(4 * rows * width * size, 2 * width * (rows + 2 * size)),
    )(*in_hbm(encoder, wk, wv))


def columns(index, count, rows, place_ref):
    if index < count - 2:
        return slice(index * rows, (index + 1) * rows)
    start = (count - 2 + ((index - count + 2) ^ place_ref[1])) * rows
    return pl.ds(pl.multiple_of(start, rows), rows)


def block_of(ref):
    return ref[(0,) * (len(ref.shape) - 2)]


def stats_kernel(place_ref, k_ref, v_ref, *refs):
    out, pieces = refs[-1], refs[:-1]
    count = len(pieces) // 2
    for index in range(count):
        query, cotangent = block_of(pieces[index]), block_of(pieces[count + index])
        cols = columns(index, count, query.shape[0], place_ref)
        scores = dot(block_of(k_ref), query, NT)
        peak = jnp.max(scores, axis=0, keepdims=True)
        shifted = jnp.exp(scores - peak)
        dprobs = dot(block_of(v_ref), cotangent, NT)
        out[0:1, cols] = peak
        out[1:2, cols] = jnp.sum(shifted, axis=0, keepdims=True)
        out[2:3, cols] = jnp.sum(shifted * dprobs, axis=0, keepdims=True)
        out[3:4, cols] = jnp.zeros_like(peak)


def whole(shape):
    return pl.BlockSpec(shape, lambda i, *place: (0,) * len(shape))


def block_at(array, index):
    if len(array.shape) == 4:
        return pl.BlockSpec((1, 1) + array.shape[2:], lambda i, place: (place[0], index, 0, 0))
    return pl.BlockSpec((1,) + array.shape[1:], lambda i, place: (index, 0, 0))


def row_stats(place, keys, values, pieces):
    enc_rows, size = keys.shape[1:]
    total = pieces[0][0].shape[-2] * len(pieces) // 2
    return pl.pallas_call(
        stats_kernel,
        grid_spec=pltpu.PrefetchScalarGridSpec(
            num_scalar_prefetch=1,
            grid=(1,),
            in_specs=[block_at(*piece) for piece in [(keys, 0), (values, 0), *pieces]],
            out_specs=whole((4, total)),
        ),
        out_shape=jax.ShapeDtypeStruct((4, total), F32),
        compiler_params=params(),
        cost_estimate=cost(
            4 * enc_rows * total * size, 4 * size * (enc_rows + total), enc_rows * total
        ),
    )(place, keys, values, *[array for array, _ in pieces])


def grads_kernel(count, place_ref, k_ref, v_ref, *refs):
    queries, cotangents, refs = refs[:count], refs[count : 2 * count], refs[2 * count :]
    stats, refs, (dk_ref, dv_ref) = refs[: -2 * PARTS - 2], refs[-2 * PARTS - 2 : -2], refs[-2:]
    keys, values = block_of(k_ref), block_of(v_ref)
    rows = refs[0].shape[1]
    for index in range(count):
        query, cotangent = block_of(queries[index]), block_of(cotangents[index])
        cols = columns(index, count, query.shape[0], place_ref)
        parts = [part[:, cols] for part in stats]
        peak = functools.reduce(jnp.maximum, [part[0:1] for part in parts])
        scales = [jnp.exp(part[0:1] - peak) for part in parts]
        total = sum(part[1:2] * scale for part, scale in zip(parts, scales))
        inner = sum(part[2:3] * scale for part, scale in zip(parts, scales)) / total
        attention = jnp.exp(dot(keys, query, NT) - peak) * (1.0 / total)
        dprobs = dot(values, cotangent, NT)
        dscores = (attention * (dprobs - inner)).astype(BF16)
        query_grad = dot(dscores, keys, TN).astype(BF16)
        slot = index if index < count - 2 else count - 2 + ((index - count + 2) ^ place_ref[1])
        first = place_ref[2] != 0
        for part in range(PARTS):
            upper = query_grad[part * rows : (part + 1) * rows]
            lower = query_grad[(PARTS + part) * rows : (PARTS + part + 1) * rows]
            refs[part][slot] = jnp.where(first, upper, lower)
            refs[PARTS + part][slot] = jnp.where(first, lower, upper)
        key_part = dot(dscores, query, NN)
        value_part = dot(attention.astype(BF16), cotangent, NN)
        key_sum = key_part if index == 0 else key_sum + key_part
        value_sum = value_part if index == 0 else value_sum + value_part
    dk_ref[...] = key_sum.astype(BF16)
    dv_ref[...] = value_sum.astype(BF16)


def attention_grads(place, keys, values, pieces, stats):
    enc_rows, size = keys.shape[1:]
    rows = pieces[0][0].shape[-2]
    count = len(pieces) // 2
    total = rows * count
    outs = [(count, rows // (2 * PARTS), size)] * (2 * PARTS) + [(enc_rows, size)] * 2
    return pl.pallas_call(
        functools.partial(grads_kernel, count),
        grid_spec=pltpu.PrefetchScalarGridSpec(
            num_scalar_prefetch=1,
            grid=(1,),
            in_specs=[block_at(*piece) for piece in [(keys, 0), (values, 0), *pieces]]
            + [whole((4, total))] * len(stats),
            out_specs=[whole(shape) for shape in outs],
        ),
        out_shape=[jax.ShapeDtypeStruct(shape, BF16) for shape in outs],
        compiler_params=params(),
        cost_estimate=cost(
            10 * enc_rows * total * size, 6 * size * (enc_rows + total), enc_rows * total
        ),
    )(place, keys, values, *[array for array, _ in pieces], *stats)


def back_kernel(order_ref, wk_ref, wv_ref, *refs):
    flat, out = refs[:-1], refs[-1]
    total = None
    for layer in range(wk_ref.shape[0]):
        part = dot(flat[2 * layer][...], wk_ref[layer], NT) + dot(flat[2 * layer + 1][...], wv_ref[layer], NT)
        total = part if total is None else total + part
    out[0] = total.astype(out.dtype)


def back_blocks(order, wk, wv, flat, share, dtype):
    layers, _, size = wk.shape
    rows = flat[0].shape[0]
    blocks = order.shape[0]
    weight = pl.BlockSpec((layers, share, size), lambda i, order: (0, order[i], 0))
    return pl.pallas_call(
        back_kernel,
        grid_spec=pltpu.PrefetchScalarGridSpec(
            num_scalar_prefetch=1,
            grid=(blocks,),
            in_specs=[weight, weight] + [pl.BlockSpec((rows, size), lambda i, order: (0, 0))] * len(flat),
            out_specs=pl.BlockSpec((1, rows, share), lambda i, order: (i, 0, 0)),
        ),
        out_shape=jax.ShapeDtypeStruct((blocks, rows, share), dtype),
        compiler_params=params(),
        cost_estimate=cost(
            4 * layers * rows * size * share * blocks, 2 * blocks * share * (2 * layers * size + 2 * rows)
        ),
    )(order, *in_hbm(wk, wv), *flat)


def plus_kernel(one_ref, two_ref, *outs):
    total = (one_ref[...].astype(F32) + two_ref[...].astype(F32)).astype(BF16)
    for index, out in enumerate(outs):
        out[...] = total if len(outs) == 1 else total[index]


def plus(one, two, spread=False):
    shape = one.shape[1:] if spread else one.shape
    outs = [jax.ShapeDtypeStruct(shape, BF16)] * (one.shape[0] if spread else 1)
    results = pl.pallas_call(
        plus_kernel,
        grid=(1,),
        in_specs=[whole(one.shape)] * 2,
        out_specs=[whole(shape)] * len(outs),
        out_shape=outs,
        compiler_params=params(),
        cost_estimate=cost(one.size, 6 * one.size),
    )(one, two)
    return results if spread else results[0]


def stack_kernel(*refs):
    for index, ref in enumerate(refs[:-1]):
        refs[-1][index] = ref[...]


def stacked(parts):
    shape = (len(parts),) + parts[0].shape
    return pl.pallas_call(
        stack_kernel,
        grid=(1,),
        in_specs=[whole(parts[0].shape)] * len(parts),
        out_specs=whole(shape),
        out_shape=jax.ShapeDtypeStruct(shape, BF16),
        compiler_params=params(),
        cost_estimate=cost(0, 4 * len(parts) * parts[0].size),
    )(*parts)


def total_kernel(*refs):
    total = refs[0][0].astype(F32)
    for ref in refs[1:-1]:
        total = total + ref[0].astype(F32)
    refs[-1][0] = total.astype(BF16)


def total_of(parts):
    shape = (1,) + parts[0][0].shape[1:]
    return pl.pallas_call(
        total_kernel,
        grid=(1,),
        in_specs=[pl.BlockSpec(shape, lambda i, index=index: (index, 0, 0)) for _, index in parts],
        out_specs=whole(shape),
        out_shape=jax.ShapeDtypeStruct(shape, BF16),
        compiler_params=params(),
        cost_estimate=cost(0, 0),
    )(*[array for array, _ in parts])


def exchange(value, n_inp, n_tgt, mask_of):
    pairs = [(z * n_tgt + t, z * n_tgt + (t ^ mask_of(z))) for z in range(n_inp) for t in range(n_tgt)]
    return lax.ppermute(value, ("inp", "tgt"), pairs)


def everywhere(value, n_inp):
    return [value] + [
        lax.ppermute(value, "inp", partners(n_inp, mask)) for mask in range(1, n_inp)
    ]


def after(value, *others):
    return lax.optimization_barrier((value, *others))[0]


def to_owners(parts, n_tgt):
    return stacked(
        [part if mask == 0 else lax.ppermute(part, "tgt", partners(n_tgt, mask)) for mask, part in enumerate(parts)]
    )


def body(encoder, key_weight, value_weight, queries, grad_out):
    layers, dec_rows, heads, size = queries.shape
    width = encoder.shape[1]
    n_inp, n_tgt, n_mdl = (lax.axis_size(axis) for axis in ("inp", "tgt", "mdl"))
    z, t, m = (lax.axis_index(axis) for axis in ("inp", "tgt", "mdl"))
    share = width // (n_tgt * n_mdl)
    wk = key_weight.reshape(layers, width, size)
    wv = value_weight.reshape(layers, width, size)
    line = n_inp == 4
    odd = (z % 2).astype(jnp.int32)
    upper = ((z == 0) | (z == n_inp - 1)).astype(jnp.int32) if line else jnp.ones_like(odd)
    place = jnp.stack([t.astype(jnp.int32), odd, upper])
    plain = jnp.stack([t.astype(jnp.int32), jnp.zeros_like(odd), upper])
    wanted_head, beside_head, heads_along = (t ^ (2 + odd))[None], (t ^ 1)[None], [(t ^ 2)[None], (t ^ 3)[None]]
    orders = [
        jnp.stack([(t ^ mask) * n_mdl + (m ^ side) for mask in masks for side in range(n_mdl)]).astype(jnp.int32)
        for masks in ((3, 1), (2, 0))
    ]
    queries, place, plain, wanted_head, beside_head, heads_along, *orders = lax.optimization_barrier(
        (queries, place, plain, wanted_head, beside_head, heads_along, *orders)
    )
    places = [place] + [plain] * (layers - 1)

    own = [jnp.transpose(array, (2, 0, 1, 3)) for array in (queries, grad_out)]
    wanted = pick(wanted_head, [(source, 0, 1) for source in own], together=True)
    fetched = [exchange(wanted[0], n_inp, n_tgt, lambda z: 2 + z % 2)]
    for layer in range(1, layers):
        fetched.append([])
        for mask, head in zip((2, 3), heads_along):
            wanted += pick(after(head, *wanted), [(source, layer, 1) for source in own], together=True)
            fetched[layer].append(lax.ppermute(wanted[-1], "tgt", partners(n_tgt, mask)))
    keys, values, begun = [], [], wanted
    for layer in range(layers):
        key_block, value_block = project(after(encoder, *begun), wk, wv, layer)
        begun = fetched[:1]
        keys.append(key_block)
        values.append(value_block)
    (beside,) = pick(after(beside_head, keys[0]), [(source, 0, layers) for source in own], together=True)
    beside = lax.ppermute(beside, "tgt", partners(n_tgt, 1))
    handed = lax.ppermute(after(fetched[0], keys[0]), "inp", partners(n_inp, 1))
    along = [[fetched[0], handed]] + fetched[1:]

    pieces, stats = [], []
    for layer in range(layers):
        pieces.append(
            [
                piece
                for kind in range(2)
                for piece in (
                    (own[kind], layer),
                    (beside, kind * layers + layer),
                    (along[layer][0], kind),
                    (along[layer][1], kind),
                )
            ]
        )
    flat, keep, send = [], [], []
    pair_sums, totals, mine, other = [], [], [], []

    def pair_sum(*others):
        index = len(pair_sums)
        if not line:
            pair_sums.append(keep[index])
        else:
            arrived = lax.ppermute(send[index], "inp", partners(n_inp, 1))
            pair_sums.append(plus(after(keep[index], *others), arrived))
        return pair_sums[-1]

    def line_sum(*others):
        index = len(totals)
        if not line:
            totals.append([lax.psum(keep[index], "inp")[mask] for mask in range(n_tgt)])
            mine.append(to_owners(totals[-1], n_tgt))
            other.append(to_owners([lax.psum(send[index], "inp")[mask] for mask in range(n_tgt)], n_tgt))
        else:
            value = pair_sums[index]
            earlier = [part for total in totals[-1:] for part in total]
            arrived = lax.ppermute(after(value, *earlier), "inp", [(0, 3), (3, 0), (1, 2), (2, 1)])
            totals.append(plus(after(value, *others), arrived, spread=True))
            mine.append(to_owners(totals[-1], n_tgt))
            other.append(lax.ppermute(mine[-1], "inp", partners(n_inp, 1)))
        return totals[-1]

    for layer in range(layers):
        ready = [] if layer else [keys[1], along[1][0]]
        own_stats = row_stats(after(places[layer], *ready), keys[layer], values[layer], pieces[layer])
        stats.append(everywhere(own_stats, n_inp))
    for layer in range(layers):
        results = attention_grads(
            after(places[layer], *(flat or [stats[-1][0]])), keys[layer], values[layer], pieces[layer], stats[layer]
        )
        keep += results[:PARTS]
        send += results[PARTS : 2 * PARTS]
        flat += results[2 * PARTS :]
    send[0] = after(send[0], *stats[-1])
    chunks = len(keep)

    sent = back_blocks(orders[0], wk, wv, flat, share, BF16)
    pair_sum(sent)
    while len(pair_sums) < chunks:
        send[len(pair_sums)] = after(send[len(pair_sums)], pair_sums[-1])
        pair_sum()
    arrived = lax.ppermute(after(sent, pair_sums[0]), "tgt", partners(n_tgt, 1))
    own_blocks = back_blocks(after(orders[1], pair_sums[0]), wk, wv, flat, share, F32)
    arrived = after(arrived, pair_sums[0])
    far_own, far_other = (total_of([(own_blocks, side), (arrived, side)]) for side in range(2))
    waits = [far_own, far_other]
    far_other = lax.ppermute(far_other, "tgt", partners(n_tgt, 2))
    far_own = lax.ppermute(far_own, "tgt", partners(n_tgt, 2))
    line_sum(*waits)
    side_own = total_of([(own_blocks, 3), (arrived, 3), (far_other, 0)])
    side_own = lax.ppermute(side_own, "mdl", partners(n_mdl, 1))
    while len(totals) < chunks:
        line_sum(side_own, far_own, mine[0])
    query_grads = None
    for layer in range(layers):
        query_grads = join_heads(place, mine[layer], True, layer, layers, query_grads)
        query_grads = join_heads(place, other[layer], False, layer, layers, query_grads)
    enc_grad = total_of([(own_blocks, 2), (arrived, 2), (far_own, 0), (side_own, 0)])
    return query_grads, enc_grad[0]


def solution(mesh):
    placed = (
        P("inp", None),
        P(None, None, "mdl", "tgt", None),
        P(None, None, "mdl", "tgt", None),
        P(None, "tgt", "mdl", None),
        P(None, "tgt", "mdl", None),
    )
    return jax.shard_map(
        body,
        mesh=mesh,
        in_specs=placed,
        out_specs=(P(None, "tgt", "mdl", None), P("inp", ("tgt", "mdl"))),
        check_vma=False,
    )
```

```python
import functools

import jax
import jax.numpy as jnp
from jax import lax
from jax.experimental import pallas as pl
from jax.experimental.pallas import tpu as pltpu
from jax.sharding import PartitionSpec as P

F32, BF16 = jnp.float32, jnp.bfloat16
MIB = 1024 * 1024
PARTS = 1
NT = (((1,), (1,)), ((), ()))
NN = (((1,), (0,)), ((), ()))
TN = (((0,), (0,)), ((), ()))


def dot(left, right, dims):
    return lax.dot_general(left, right, dims, preferred_element_type=F32)


def params():
    return pltpu.CompilerParams(vmem_limit_bytes=24 * MIB)


def cost(flops, nbytes, exps=0):
    return pl.CostEstimate(flops=int(flops), bytes_accessed=int(nbytes), transcendentals=int(exps))


def in_hbm(*arrays):
    return [pltpu.with_memory_space_constraint(array, pltpu.HBM) for array in arrays]


def partners(count, mask):
    return [(index, index ^ mask) for index in range(count)]


def pick_kernel(head_ref, *refs):
    count = sum(len(ref.shape) == 4 for ref in refs)
    sources, outs = refs[:count], refs[count:]
    for index, source in enumerate(sources):
        if len(outs) == count:
            outs[index][...] = source[0]
        else:
            layers = source.shape[1]
            outs[0][index * layers : (index + 1) * layers] = source[0]


def pick(head, parts, together=False):
    shape = parts[0][0].shape
    specs, sizes = [], []
    for source, first, count in parts:
        specs.append(
            pl.BlockSpec((1, count) + shape[2:], lambda i, head, first=first: (head[0], first, 0, 0))
        )
        sizes.append(count)
    sizes = [sum(sizes)] if together else sizes
    outs = [jax.ShapeDtypeStruct((size,) + shape[2:], BF16) for size in sizes]
    return pl.pallas_call(
        pick_kernel,
        grid_spec=pltpu.PrefetchScalarGridSpec(
            num_scalar_prefetch=1,
            grid=(1,),
            in_specs=specs,
            out_specs=[pl.BlockSpec(out.shape, lambda i, head: (0, 0, 0)) for out in outs],
        ),
        out_shape=outs,
        compiler_params=params(),
        cost_estimate=cost(0, 4 * sum(out.size for out in outs)),
    )(head, *[source for source, _, _ in parts])


def join_kernel(place_ref, part_ref, *rest):
    out = rest[-1]
    for head in range(part_ref.shape[0]):
        out[0, :, head, :] = part_ref[place_ref[0] ^ head]


def join_heads(place, part, mine, layer, layers, begun):
    heads, rows, size = part.shape
    extra = [] if begun is None else [begun]

    def half(i, place):
        return (layer, (1 - place[2]) if mine else place[2], 0, 0)

    return pl.pallas_call(
        join_kernel,
        grid_spec=pltpu.PrefetchScalarGridSpec(
            num_scalar_prefetch=1,
            grid=(1,),
            in_specs=[whole(part.shape)] + [pl.BlockSpec(memory_space=pl.ANY)] * len(extra),
            out_specs=pl.BlockSpec((1, rows, heads, size), half),
        ),
        out_shape=jax.ShapeDtypeStruct((layers, 2 * rows, heads, size), BF16),
        input_output_aliases={2: 0} if extra else {},
        compiler_params=params(),
        cost_estimate=cost(0, 4 * rows * heads * size),
    )(place, part, *extra)


def project_kernel(enc_ref, wk_ref, wv_ref, k_ref, v_ref, sums):
    step = pl.program_id(0)

    @pl.when(step == 0)
    def _():
        sums[...] = jnp.zeros_like(sums)

    sums[0] += dot(enc_ref[...], wk_ref[0], NN)
    sums[1] += dot(enc_ref[...], wv_ref[0], NN)

    @pl.when(step == pl.num_programs(0) - 1)
    def _():
        k_ref[0] = sums[0].astype(BF16)
        v_ref[0] = sums[1].astype(BF16)


def project(encoder, wk, wv, layer):
    rows, width = encoder.shape
    size = wk.shape[2]
    depth = width // 4
    weight = pl.BlockSpec((1, depth, size), lambda i: (layer, i, 0))
    result = whole((1, rows, size))
    return pl.pallas_call(
        project_kernel,
        grid=(width // depth,),
        in_specs=[pl.BlockSpec((rows, depth), lambda i: (0, i)), weight, weight],
        out_specs=[result, result],
        out_shape=[jax.ShapeDtypeStruct((1, rows, size), BF16)] * 2,
        scratch_shapes=[pltpu.VMEM((2, rows, size), F32)],
        compiler_params=params(),
        cost_estimate=cost(4 * rows * width * size, 2 * width * (rows + 2 * size)),
    )(*in_hbm(encoder, wk, wv))


def columns(index, count, rows, place_ref):
    if index < count - 2:
        return slice(index * rows, (index + 1) * rows)
    start = (count - 2 + ((index - count + 2) ^ place_ref[1])) * rows
    return pl.ds(pl.multiple_of(start, rows), rows)


def block_of(ref):
    return ref[(0,) * (len(ref.shape) - 2)]


def stats_kernel(place_ref, k_ref, v_ref, *refs):
    out, pieces = refs[-1], refs[:-1]
    count = len(pieces) // 2
    for index in range(count):
        query, cotangent = block_of(pieces[index]), block_of(pieces[count + index])
        cols = columns(index, count, query.shape[0], place_ref)
        scores = dot(block_of(k_ref), query, NT)
        peak = jnp.max(scores, axis=0, keepdims=True)
        shifted = jnp.exp(scores - peak)
        dprobs = dot(block_of(v_ref), cotangent, NT)
        out[0:1, cols] = peak
        out[1:2, cols] = jnp.sum(shifted, axis=0, keepdims=True)
        out[2:3, cols] = jnp.sum(shifted * dprobs, axis=0, keepdims=True)
        out[3:4, cols] = jnp.zeros_like(peak)


def whole(shape):
    return pl.BlockSpec(shape, lambda i, *place: (0,) * len(shape))


def block_at(array, index):
    if len(array.shape) == 4:
        return pl.BlockSpec((1, 1) + array.shape[2:], lambda i, place: (place[0], index, 0, 0))
    return pl.BlockSpec((1,) + array.shape[1:], lambda i, place: (index, 0, 0))


def row_stats(place, keys, values, pieces):
    enc_rows, size = keys.shape[1:]
    total = pieces[0][0].shape[-2] * len(pieces) // 2
    return pl.pallas_call(
        stats_kernel,
        grid_spec=pltpu.PrefetchScalarGridSpec(
            num_scalar_prefetch=1,
            grid=(1,),
            in_specs=[block_at(*piece) for piece in [(keys, 0), (values, 0), *pieces]],
            out_specs=whole((4, total)),
        ),
        out_shape=jax.ShapeDtypeStruct((4, total), F32),
        compiler_params=params(),
        cost_estimate=cost(
            4 * enc_rows * total * size, 4 * size * (enc_rows + total), enc_rows * total
        ),
    )(place, keys, values, *[array for array, _ in pieces])


def grads_kernel(count, place_ref, k_ref, v_ref, *refs):
    queries, cotangents, refs = refs[:count], refs[count : 2 * count], refs[2 * count :]
    stats, refs, (dk_ref, dv_ref) = refs[: -2 * PARTS - 2], refs[-2 * PARTS - 2 : -2], refs[-2:]
    keys, values = block_of(k_ref), block_of(v_ref)
    rows = refs[0].shape[1]
    for index in range(count):
        query, cotangent = block_of(queries[index]), block_of(cotangents[index])
        cols = columns(index, count, query.shape[0], place_ref)
        parts = [part[:, cols] for part in stats]
        peak = functools.reduce(jnp.maximum, [part[0:1] for part in parts])
        scales = [jnp.exp(part[0:1] - peak) for part in parts]
        total = sum(part[1:2] * scale for part, scale in zip(parts, scales))
        inner = sum(part[2:3] * scale for part, scale in zip(parts, scales)) / total
        attention = jnp.exp(dot(keys, query, NT) - peak) * (1.0 / total)
        dprobs = dot(values, cotangent, NT)
        dscores = (attention * (dprobs - inner)).astype(BF16)
        query_grad = dot(dscores, keys, TN).astype(BF16)
        slot = index if index < count - 2 else count - 2 + ((index - count + 2) ^ place_ref[1])
        first = place_ref[2] != 0
        for part in range(PARTS):
            upper = query_grad[part * rows : (part + 1) * rows]
            lower = query_grad[(PARTS + part) * rows : (PARTS + part + 1) * rows]
            refs[part][slot] = jnp.where(first, upper, lower)
            refs[PARTS + part][slot] = jnp.where(first, lower, upper)
        key_part = dot(dscores, query, NN)
        value_part = dot(attention.astype(BF16), cotangent, NN)
        key_sum = key_part if index == 0 else key_sum + key_part
        value_sum = value_part if index == 0 else value_sum + value_part
    dk_ref[...] = key_sum.astype(BF16)
    dv_ref[...] = value_sum.astype(BF16)


def attention_grads(place, keys, values, pieces, stats):
    enc_rows, size = keys.shape[1:]
    rows = pieces[0][0].shape[-2]
    count = len(pieces) // 2
    total = rows * count
    outs = [(count, rows // (2 * PARTS), size)] * (2 * PARTS) + [(enc_rows, size)] * 2
    return pl.pallas_call(
        functools.partial(grads_kernel, count),
        grid_spec=pltpu.PrefetchScalarGridSpec(
            num_scalar_prefetch=1,
            grid=(1,),
            in_specs=[block_at(*piece) for piece in [(keys, 0), (values, 0), *pieces]]
            + [whole((4, total))] * len(stats),
            out_specs=[whole(shape) for shape in outs],
        ),
        out_shape=[jax.ShapeDtypeStruct(shape, BF16) for shape in outs],
        compiler_params=params(),
        cost_estimate=cost(
            10 * enc_rows * total * size, 6 * size * (enc_rows + total), enc_rows * total
        ),
    )(place, keys, values, *[array for array, _ in pieces], *stats)


def back_kernel(order_ref, wk_ref, wv_ref, *refs):
    flat, out = refs[:-1], refs[-1]
    total = None
    for layer in range(wk_ref.shape[0]):
        part = dot(flat[2 * layer][...], wk_ref[layer], NT) + dot(flat[2 * layer + 1][...], wv_ref[layer], NT)
        total = part if total is None else total + part
    out[0] = total.astype(out.dtype)


def back_blocks(order, wk, wv, flat, share, dtype):
    layers, _, size = wk.shape
    rows = flat[0].shape[0]
    blocks = order.shape[0]
    weight = pl.BlockSpec((layers, share, size), lambda i, order: (0, order[i], 0))
    return pl.pallas_call(
        back_kernel,
        grid_spec=pltpu.PrefetchScalarGridSpec(
            num_scalar_prefetch=1,
            grid=(blocks,),
            in_specs=[weight, weight] + [pl.BlockSpec((rows, size), lambda i, order: (0, 0))] * len(flat),
            out_specs=pl.BlockSpec((1, rows, share), lambda i, order: (i, 0, 0)),
        ),
        out_shape=jax.ShapeDtypeStruct((blocks, rows, share), dtype),
        compiler_params=params(),
        cost_estimate=cost(
            4 * layers * rows * size * share * blocks, 2 * blocks * share * (2 * layers * size + 2 * rows)
        ),
    )(order, *in_hbm(wk, wv), *flat)


def plus_kernel(one_ref, two_ref, *outs):
    total = (one_ref[...].astype(F32) + two_ref[...].astype(F32)).astype(BF16)
    for index, out in enumerate(outs):
        out[...] = total if len(outs) == 1 else total[index]


def plus(one, two, spread=False):
    shape = one.shape[1:] if spread else one.shape
    outs = [jax.ShapeDtypeStruct(shape, BF16)] * (one.shape[0] if spread else 1)
    results = pl.pallas_call(
        plus_kernel,
        grid=(1,),
        in_specs=[whole(one.shape)] * 2,
        out_specs=[whole(shape)] * len(outs),
        out_shape=outs,
        compiler_params=params(),
        cost_estimate=cost(one.size, 6 * one.size),
    )(one, two)
    return results if spread else results[0]


def stack_kernel(*refs):
    for index, ref in enumerate(refs[:-1]):
        refs[-1][index] = ref[...]


def stacked(parts):
    shape = (len(parts),) + parts[0].shape
    return pl.pallas_call(
        stack_kernel,
        grid=(1,),
        in_specs=[whole(parts[0].shape)] * len(parts),
        out_specs=whole(shape),
        out_shape=jax.ShapeDtypeStruct(shape, BF16),
        compiler_params=params(),
        cost_estimate=cost(0, 4 * len(parts) * parts[0].size),
    )(*parts)


def total_kernel(*refs):
    total = refs[0][0].astype(F32)
    for ref in refs[1:-1]:
        total = total + ref[0].astype(F32)
    refs[-1][0] = total.astype(BF16)


def total_of(parts):
    shape = (1,) + parts[0][0].shape[1:]
    return pl.pallas_call(
        total_kernel,
        grid=(1,),
        in_specs=[pl.BlockSpec(shape, lambda i, index=index: (index, 0, 0)) for _, index in parts],
        out_specs=whole(shape),
        out_shape=jax.ShapeDtypeStruct(shape, BF16),
        compiler_params=params(),
        cost_estimate=cost(0, 0),
    )(*[array for array, _ in parts])


def exchange(value, n_inp, n_tgt, mask_of):
    pairs = [(z * n_tgt + t, z * n_tgt + (t ^ mask_of(z))) for z in range(n_inp) for t in range(n_tgt)]
    return lax.ppermute(value, ("inp", "tgt"), pairs)


def everywhere(value, n_inp):
    return [value] + [
        lax.ppermute(value, "inp", partners(n_inp, mask)) for mask in range(1, n_inp)
    ]


def after(value, *others):
    return lax.optimization_barrier((value, *others))[0]


def to_owners(parts, n_tgt):
    return stacked(
        [part if mask == 0 else lax.ppermute(part, "tgt", partners(n_tgt, mask)) for mask, part in enumerate(parts)]
    )


def body(encoder, key_weight, value_weight, queries, grad_out):
    layers, dec_rows, heads, size = queries.shape
    width = encoder.shape[1]
    n_inp, n_tgt, n_mdl = (lax.axis_size(axis) for axis in ("inp", "tgt", "mdl"))
    z, t, m = (lax.axis_index(axis) for axis in ("inp", "tgt", "mdl"))
    share = width // (n_tgt * n_mdl)
    wk = key_weight.reshape(layers, width, size)
    wv = value_weight.reshape(layers, width, size)
    line = n_inp == 4
    odd = (z % 2).astype(jnp.int32)
    upper = ((z == 0) | (z == n_inp - 1)).astype(jnp.int32) if line else jnp.ones_like(odd)
    place = jnp.stack([t.astype(jnp.int32), odd, upper])
    plain = jnp.stack([t.astype(jnp.int32), jnp.zeros_like(odd), upper])
    wanted_head, beside_head, heads_along = (t ^ (2 + odd))[None], (t ^ 1)[None], [(t ^ 2)[None], (t ^ 3)[None]]
    orders = [
        jnp.stack([(t ^ mask) * n_mdl + (m ^ side) for mask in masks for side in range(n_mdl)]).astype(jnp.int32)
        for masks in ((3, 1), (2, 0))
    ]
    queries, place, plain, wanted_head, beside_head, heads_along, *orders = lax.optimization_barrier(
        (queries, place, plain, wanted_head, beside_head, heads_along, *orders)
    )
    places = [place] + [plain] * (layers - 1)

    own = [jnp.transpose(array, (2, 0, 1, 3)) for array in (queries, grad_out)]
    wanted = pick(wanted_head, [(source, 0, 1) for source in own], together=True)
    fetched = [exchange(wanted[0], n_inp, n_tgt, lambda z: 2 + z % 2)]
    for layer in range(1, layers):
        fetched.append([])
        for mask, head in zip((2, 3), heads_along):
            wanted += pick(after(head, *wanted), [(source, layer, 1) for source in own], together=True)
            fetched[layer].append(lax.ppermute(wanted[-1], "tgt", partners(n_tgt, mask)))
    keys, values, begun = [], [], wanted
    for layer in range(layers):
        key_block, value_block = project(after(encoder, *begun), wk, wv, layer)
        begun = fetched[:1]
        keys.append(key_block)
        values.append(value_block)
    (beside,) = pick(after(beside_head, keys[0]), [(source, 0, layers) for source in own], together=True)
    beside = lax.ppermute(beside, "tgt", partners(n_tgt, 1))
    handed = lax.ppermute(after(fetched[0], keys[0]), "inp", partners(n_inp, 1))
    along = [[fetched[0], handed]] + fetched[1:]

    pieces, stats = [], []
    for layer in range(layers):
        pieces.append(
            [
                piece
                for kind in range(2)
                for piece in (
                    (own[kind], layer),
                    (beside, kind * layers + layer),
                    (along[layer][0], kind),
                    (along[layer][1], kind),
                )
            ]
        )
    flat, keep, send = [], [], []
    pair_sums, totals, mine, other = [], [], [], []

    def pair_sum(*others):
        index = len(pair_sums)
        if not line:
            pair_sums.append(keep[index])
        else:
            arrived = lax.ppermute(send[index], "inp", partners(n_inp, 1))
            pair_sums.append(plus(after(keep[index], *others), arrived))
        return pair_sums[-1]

    def line_sum(*others):
        index = len(totals)
        if not line:
            totals.append([lax.psum(keep[index], "inp")[mask] for mask in range(n_tgt)])
            mine.append(to_owners(totals[-1], n_tgt))
            other.append(to_owners([lax.psum(send[index], "inp")[mask] for mask in range(n_tgt)], n_tgt))
        else:
            value = pair_sums[index]
            earlier = [part for total in totals[-1:] for part in total]
            arrived = lax.ppermute(after(value, *earlier), "inp", [(0, 3), (3, 0), (1, 2), (2, 1)])
            totals.append(plus(after(value, *others), arrived, spread=True))
            mine.append(to_owners(totals[-1], n_tgt))
            other.append(lax.ppermute(mine[-1], "inp", partners(n_inp, 1)))
        return totals[-1]

    for layer in range(layers):
        ready = [] if layer else [keys[1], along[1][0]]
        own_stats = row_stats(after(places[layer], *ready), keys[layer], values[layer], pieces[layer])
        stats.append(everywhere(own_stats, n_inp))
    for layer in range(layers):
        results = attention_grads(
            after(places[layer], *(flat or [stats[-1][0]])), keys[layer], values[layer], pieces[layer], stats[layer]
        )
        keep += results[:PARTS]
        send += results[PARTS : 2 * PARTS]
        flat += results[2 * PARTS :]
    send[0] = after(send[0], *stats[-1])
    chunks = len(keep)

    sent = back_blocks(orders[0], wk, wv, flat, share, BF16)
    pair_sum(sent)
    while len(pair_sums) < chunks:
        send[len(pair_sums)] = after(send[len(pair_sums)], pair_sums[-1])
        pair_sum()
    arrived = lax.ppermute(after(sent, pair_sums[0]), "tgt", partners(n_tgt, 1))
    own_blocks = back_blocks(after(orders[1], pair_sums[0]), wk, wv, flat, share, F32)
    arrived = after(arrived, pair_sums[0])
    far_own, far_other = (total_of([(own_blocks, side), (arrived, side)]) for side in range(2))
    waits = [far_own, far_other]
    far_other = lax.ppermute(far_other, "tgt", partners(n_tgt, 2))
    far_own = lax.ppermute(far_own, "tgt", partners(n_tgt, 2))
    line_sum(*waits)
    side_own = total_of([(own_blocks, 3), (arrived, 3), (after(far_other, mine[0]), 0)])
    side_own = lax.ppermute(side_own, "mdl", partners(n_mdl, 1))
    while len(totals) < chunks:
        line_sum(far_own, mine[0])
    query_grads = None
    for layer in range(layers):
        query_grads = join_heads(place, mine[layer], True, layer, layers, query_grads)
        query_grads = join_heads(place, other[layer], False, layer, layers, query_grads)
    enc_grad = total_of([(own_blocks, 2), (arrived, 2), (far_own, 0), (side_own, 0)])
    return query_grads, enc_grad[0]


def solution(mesh):
    placed = (
        P("inp", None),
        P(None, None, "mdl", "tgt", None),
        P(None, None, "mdl", "tgt", None),
        P(None, "tgt", "mdl", None),
        P(None, "tgt", "mdl", None),
    )
    return jax.shard_map(
        body,
        mesh=mesh,
        in_specs=placed,
        out_specs=(P(None, "tgt", "mdl", None), P("inp", ("tgt", "mdl"))),
        check_vma=False,
    )
```

```python
import functools

import jax
import jax.numpy as jnp
from jax import lax
from jax.experimental import pallas as pl
from jax.experimental.pallas import tpu as pltpu
from jax.sharding import PartitionSpec as P

F32, BF16 = jnp.float32, jnp.bfloat16
MIB = 1024 * 1024
PARTS = 1
NT = (((1,), (1,)), ((), ()))
NN = (((1,), (0,)), ((), ()))
TN = (((0,), (0,)), ((), ()))


def dot(left, right, dims):
    return lax.dot_general(left, right, dims, preferred_element_type=F32)


def params():
    return pltpu.CompilerParams(vmem_limit_bytes=24 * MIB)


def cost(flops, nbytes, exps=0):
    return pl.CostEstimate(flops=int(flops), bytes_accessed=int(nbytes), transcendentals=int(exps))


def in_hbm(*arrays):
    return [pltpu.with_memory_space_constraint(array, pltpu.HBM) for array in arrays]


def partners(count, mask):
    return [(index, index ^ mask) for index in range(count)]


def pick_kernel(head_ref, *refs):
    count = sum(len(ref.shape) == 4 for ref in refs)
    sources, outs = refs[:count], refs[count:]
    for index, source in enumerate(sources):
        if len(outs) == count:
            outs[index][...] = source[0]
        else:
            layers = source.shape[1]
            outs[0][index * layers : (index + 1) * layers] = source[0]


def pick(head, parts, together=False):
    shape = parts[0][0].shape
    specs, sizes = [], []
    for source, first, count in parts:
        specs.append(
            pl.BlockSpec((1, count) + shape[2:], lambda i, head, first=first: (head[0], first, 0, 0))
        )
        sizes.append(count)
    sizes = [sum(sizes)] if together else sizes
    outs = [jax.ShapeDtypeStruct((size,) + shape[2:], BF16) for size in sizes]
    return pl.pallas_call(
        pick_kernel,
        grid_spec=pltpu.PrefetchScalarGridSpec(
            num_scalar_prefetch=1,
            grid=(1,),
            in_specs=specs,
            out_specs=[pl.BlockSpec(out.shape, lambda i, head: (0, 0, 0)) for out in outs],
        ),
        out_shape=outs,
        compiler_params=params(),
        cost_estimate=cost(0, 4 * sum(out.size for out in outs)),
    )(head, *[source for source, _, _ in parts])


def join_kernel(place_ref, part_ref, *rest):
    out = rest[-1]
    for head in range(part_ref.shape[0]):
        out[0, :, head, :] = part_ref[place_ref[0] ^ head]


def join_heads(place, part, mine, layer, layers, begun):
    heads, rows, size = part.shape
    extra = [] if begun is None else [begun]

    def half(i, place):
        return (layer, (1 - place[2]) if mine else place[2], 0, 0)

    return pl.pallas_call(
        join_kernel,
        grid_spec=pltpu.PrefetchScalarGridSpec(
            num_scalar_prefetch=1,
            grid=(1,),
            in_specs=[whole(part.shape)] + [pl.BlockSpec(memory_space=pl.ANY)] * len(extra),
            out_specs=pl.BlockSpec((1, rows, heads, size), half),
        ),
        out_shape=jax.ShapeDtypeStruct((layers, 2 * rows, heads, size), BF16),
        input_output_aliases={2: 0} if extra else {},
        compiler_params=params(),
        cost_estimate=cost(0, 4 * rows * heads * size),
    )(place, part, *extra)


def project_kernel(enc_ref, wk_ref, wv_ref, k_ref, v_ref, sums):
    step = pl.program_id(0)

    @pl.when(step == 0)
    def _():
        sums[...] = jnp.zeros_like(sums)

    sums[0] += dot(enc_ref[...], wk_ref[0], NN)
    sums[1] += dot(enc_ref[...], wv_ref[0], NN)

    @pl.when(step == pl.num_programs(0) - 1)
    def _():
        k_ref[0] = sums[0].astype(BF16)
        v_ref[0] = sums[1].astype(BF16)


def project(encoder, wk, wv, layer):
    rows, width = encoder.shape
    size = wk.shape[2]
    depth = width // 4
    weight = pl.BlockSpec((1, depth, size), lambda i: (layer, i, 0))
    result = whole((1, rows, size))
    return pl.pallas_call(
        project_kernel,
        grid=(width // depth,),
        in_specs=[pl.BlockSpec((rows, depth), lambda i: (0, i)), weight, weight],
        out_specs=[result, result],
        out_shape=[jax.ShapeDtypeStruct((1, rows, size), BF16)] * 2,
        scratch_shapes=[pltpu.VMEM((2, rows, size), F32)],
        compiler_params=params(),
        cost_estimate=cost(4 * rows * width * size, 2 * width * (rows + 2 * size)),
    )(*in_hbm(encoder, wk, wv))


def columns(index, count, rows, place_ref):
    if index < count - 2:
        return slice(index * rows, (index + 1) * rows)
    start = (count - 2 + ((index - count + 2) ^ place_ref[1])) * rows
    return pl.ds(pl.multiple_of(start, rows), rows)


def block_of(ref):
    return ref[(0,) * (len(ref.shape) - 2)]


def stats_kernel(place_ref, k_ref, v_ref, *refs):
    out, pieces = refs[-1], refs[:-1]
    count = len(pieces) // 2
    for index in range(count):
        query, cotangent = block_of(pieces[index]), block_of(pieces[count + index])
        cols = columns(index, count, query.shape[0], place_ref)
        scores = dot(block_of(k_ref), query, NT)
        peak = jnp.max(scores, axis=0, keepdims=True)
        shifted = jnp.exp(scores - peak)
        dprobs = dot(block_of(v_ref), cotangent, NT)
        out[0:1, cols] = peak
        out[1:2, cols] = jnp.sum(shifted, axis=0, keepdims=True)
        out[2:3, cols] = jnp.sum(shifted * dprobs, axis=0, keepdims=True)
        out[3:4, cols] = jnp.zeros_like(peak)


def whole(shape):
    return pl.BlockSpec(shape, lambda i, *place: (0,) * len(shape))


def block_at(array, index):
    if len(array.shape) == 4:
        return pl.BlockSpec((1, 1) + array.shape[2:], lambda i, place: (place[0], index, 0, 0))
    return pl.BlockSpec((1,) + array.shape[1:], lambda i, place: (index, 0, 0))


def row_stats(place, keys, values, pieces):
    enc_rows, size = keys.shape[1:]
    total = pieces[0][0].shape[-2] * len(pieces) // 2
    return pl.pallas_call(
        stats_kernel,
        grid_spec=pltpu.PrefetchScalarGridSpec(
            num_scalar_prefetch=1,
            grid=(1,),
            in_specs=[block_at(*piece) for piece in [(keys, 0), (values, 0), *pieces]],
            out_specs=whole((4, total)),
        ),
        out_shape=jax.ShapeDtypeStruct((4, total), F32),
        compiler_params=params(),
        cost_estimate=cost(
            4 * enc_rows * total * size, 4 * size * (enc_rows + total), enc_rows * total
        ),
    )(place, keys, values, *[array for array, _ in pieces])


def grads_kernel(count, place_ref, k_ref, v_ref, *refs):
    queries, cotangents, refs = refs[:count], refs[count : 2 * count], refs[2 * count :]
    stats, refs, (dk_ref, dv_ref) = refs[: -2 * PARTS - 2], refs[-2 * PARTS - 2 : -2], refs[-2:]
    keys, values = block_of(k_ref), block_of(v_ref)
    rows = refs[0].shape[1]
    for index in range(count):
        query, cotangent = block_of(queries[index]), block_of(cotangents[index])
        cols = columns(index, count, query.shape[0], place_ref)
        parts = [part[:, cols] for part in stats]
        peak = functools.reduce(jnp.maximum, [part[0:1] for part in parts])
        scales = [jnp.exp(part[0:1] - peak) for part in parts]
        total = sum(part[1:2] * scale for part, scale in zip(parts, scales))
        inner = sum(part[2:3] * scale for part, scale in zip(parts, scales)) / total
        attention = jnp.exp(dot(keys, query, NT) - peak) * (1.0 / total)
        dprobs = dot(values, cotangent, NT)
        dscores = (attention * (dprobs - inner)).astype(BF16)
        query_grad = dot(dscores, keys, TN).astype(BF16)
        slot = index if index < count - 2 else count - 2 + ((index - count + 2) ^ place_ref[1])
        first = place_ref[2] != 0
        for part in range(PARTS):
            upper = query_grad[part * rows : (part + 1) * rows]
            lower = query_grad[(PARTS + part) * rows : (PARTS + part + 1) * rows]
            refs[part][slot] = jnp.where(first, upper, lower)
            refs[PARTS + part][slot] = jnp.where(first, lower, upper)
        key_part = dot(dscores, query, NN)
        value_part = dot(attention.astype(BF16), cotangent, NN)
        key_sum = key_part if index == 0 else key_sum + key_part
        value_sum = value_part if index == 0 else value_sum + value_part
    dk_ref[...] = key_sum.astype(BF16)
    dv_ref[...] = value_sum.astype(BF16)


def attention_grads(place, keys, values, pieces, stats):
    enc_rows, size = keys.shape[1:]
    rows = pieces[0][0].shape[-2]
    count = len(pieces) // 2
    total = rows * count
    outs = [(count, rows // (2 * PARTS), size)] * (2 * PARTS) + [(enc_rows, size)] * 2
    return pl.pallas_call(
        functools.partial(grads_kernel, count),
        grid_spec=pltpu.PrefetchScalarGridSpec(
            num_scalar_prefetch=1,
            grid=(1,),
            in_specs=[block_at(*piece) for piece in [(keys, 0), (values, 0), *pieces]]
            + [whole((4, total))] * len(stats),
            out_specs=[whole(shape) for shape in outs],
        ),
        out_shape=[jax.ShapeDtypeStruct(shape, BF16) for shape in outs],
        compiler_params=params(),
        cost_estimate=cost(
            10 * enc_rows * total * size, 6 * size * (enc_rows + total), enc_rows * total
        ),
    )(place, keys, values, *[array for array, _ in pieces], *stats)


def back_kernel(order_ref, wk_ref, wv_ref, *refs):
    flat, out = refs[:-1], refs[-1]
    total = None
    for layer in range(wk_ref.shape[0]):
        part = dot(flat[2 * layer][...], wk_ref[layer], NT) + dot(flat[2 * layer + 1][...], wv_ref[layer], NT)
        total = part if total is None else total + part
    out[0] = total.astype(out.dtype)


def back_blocks(order, wk, wv, flat, share, dtype):
    layers, _, size = wk.shape
    rows = flat[0].shape[0]
    blocks = order.shape[0]
    weight = pl.BlockSpec((layers, share, size), lambda i, order: (0, order[i], 0))
    return pl.pallas_call(
        back_kernel,
        grid_spec=pltpu.PrefetchScalarGridSpec(
            num_scalar_prefetch=1,
            grid=(blocks,),
            in_specs=[weight, weight] + [pl.BlockSpec((rows, size), lambda i, order: (0, 0))] * len(flat),
            out_specs=pl.BlockSpec((1, rows, share), lambda i, order: (i, 0, 0)),
        ),
        out_shape=jax.ShapeDtypeStruct((blocks, rows, share), dtype),
        compiler_params=params(),
        cost_estimate=cost(
            4 * layers * rows * size * share * blocks, 2 * blocks * share * (2 * layers * size + 2 * rows)
        ),
    )(order, *in_hbm(wk, wv), *flat)


def plus_kernel(one_ref, two_ref, *outs):
    total = (one_ref[...].astype(F32) + two_ref[...].astype(F32)).astype(BF16)
    for index, out in enumerate(outs):
        out[...] = total if len(outs) == 1 else total[index]


def plus(one, two, spread=False):
    shape = one.shape[1:] if spread else one.shape
    outs = [jax.ShapeDtypeStruct(shape, BF16)] * (one.shape[0] if spread else 1)
    results = pl.pallas_call(
        plus_kernel,
        grid=(1,),
        in_specs=[whole(one.shape)] * 2,
        out_specs=[whole(shape)] * len(outs),
        out_shape=outs,
        compiler_params=params(),
        cost_estimate=cost(one.size, 6 * one.size),
    )(one, two)
    return results if spread else results[0]


def stack_kernel(*refs):
    for index, ref in enumerate(refs[:-1]):
        refs[-1][index] = ref[...]


def stacked(parts):
    shape = (len(parts),) + parts[0].shape
    return pl.pallas_call(
        stack_kernel,
        grid=(1,),
        in_specs=[whole(parts[0].shape)] * len(parts),
        out_specs=whole(shape),
        out_shape=jax.ShapeDtypeStruct(shape, BF16),
        compiler_params=params(),
        cost_estimate=cost(0, 4 * len(parts) * parts[0].size),
    )(*parts)


def total_kernel(*refs):
    total = refs[0][0].astype(F32)
    for ref in refs[1:-1]:
        total = total + ref[0].astype(F32)
    refs[-1][0] = total.astype(BF16)


def total_of(parts):
    shape = (1,) + parts[0][0].shape[1:]
    return pl.pallas_call(
        total_kernel,
        grid=(1,),
        in_specs=[pl.BlockSpec(shape, lambda i, index=index: (index, 0, 0)) for _, index in parts],
        out_specs=whole(shape),
        out_shape=jax.ShapeDtypeStruct(shape, BF16),
        compiler_params=params(),
        cost_estimate=cost(0, 0),
    )(*[array for array, _ in parts])


def exchange(value, n_inp, n_tgt, mask_of):
    pairs = [(z * n_tgt + t, z * n_tgt + (t ^ mask_of(z))) for z in range(n_inp) for t in range(n_tgt)]
    return lax.ppermute(value, ("inp", "tgt"), pairs)


def everywhere(value, n_inp):
    return [value] + [
        lax.ppermute(value, "inp", partners(n_inp, mask)) for mask in range(1, n_inp)
    ]


def after(value, *others):
    return lax.optimization_barrier((value, *others))[0]


def to_owners(parts, n_tgt):
    return stacked(
        [part if mask == 0 else lax.ppermute(part, "tgt", partners(n_tgt, mask)) for mask, part in enumerate(parts)]
    )


def body(encoder, key_weight, value_weight, queries, grad_out):
    layers, dec_rows, heads, size = queries.shape
    width = encoder.shape[1]
    n_inp, n_tgt, n_mdl = (lax.axis_size(axis) for axis in ("inp", "tgt", "mdl"))
    z, t, m = (lax.axis_index(axis) for axis in ("inp", "tgt", "mdl"))
    share = width // (n_tgt * n_mdl)
    wk = key_weight.reshape(layers, width, size)
    wv = value_weight.reshape(layers, width, size)
    line = n_inp == 4
    odd = (z % 2).astype(jnp.int32)
    upper = ((z == 0) | (z == n_inp - 1)).astype(jnp.int32) if line else jnp.ones_like(odd)
    place = jnp.stack([t.astype(jnp.int32), odd, upper])
    plain = jnp.stack([t.astype(jnp.int32), jnp.zeros_like(odd), upper])
    wanted_head, beside_head, heads_along = (t ^ (2 + odd))[None], (t ^ 1)[None], [(t ^ 2)[None], (t ^ 3)[None]]
    orders = [
        jnp.stack([(t ^ mask) * n_mdl + (m ^ side) for mask in masks for side in range(n_mdl)]).astype(jnp.int32)
        for masks in ((3, 1), (2, 0))
    ]
    queries, place, plain, wanted_head, beside_head, heads_along, *orders = lax.optimization_barrier(
        (queries, place, plain, wanted_head, beside_head, heads_along, *orders)
    )
    places = [place] + [plain] * (layers - 1)

    own = [jnp.transpose(array, (2, 0, 1, 3)) for array in (queries, grad_out)]
    wanted = pick(wanted_head, [(source, 0, 1) for source in own], together=True)
    fetched = [exchange(wanted[0], n_inp, n_tgt, lambda z: 2 + z % 2)]
    for layer in range(1, layers):
        fetched.append([])
        for mask, head in zip((2, 3), heads_along):
            wanted += pick(after(head, *wanted), [(source, layer, 1) for source in own], together=True)
            fetched[layer].append(lax.ppermute(wanted[-1], "tgt", partners(n_tgt, mask)))
    keys, values, begun = [], [], wanted
    for layer in range(layers):
        key_block, value_block = project(after(encoder, *begun), wk, wv, layer)
        begun = fetched[:1]
        keys.append(key_block)
        values.append(value_block)
    (beside,) = pick(after(beside_head, keys[0]), [(source, 0, layers) for source in own], together=True)
    beside = lax.ppermute(beside, "tgt", partners(n_tgt, 1))
    handed = lax.ppermute(after(fetched[0], keys[0]), "inp", partners(n_inp, 1))
    along = [[fetched[0], handed]] + fetched[1:]

    pieces, stats = [], []
    for layer in range(layers):
        pieces.append(
            [
                piece
                for kind in range(2)
                for piece in (
                    (own[kind], layer),
                    (beside, kind * layers + layer),
                    (along[layer][0], kind),
                    (along[layer][1], kind),
                )
            ]
        )
    flat, keep, send = [], [], []
    pair_sums, totals, mine, other = [], [], [], []

    def pair_sum(*others):
        index = len(pair_sums)
        if not line:
            pair_sums.append(keep[index])
        else:
            arrived = lax.ppermute(send[index], "inp", partners(n_inp, 1))
            pair_sums.append(plus(after(keep[index], *others), arrived))
        return pair_sums[-1]

    def line_sum(*others):
        index = len(totals)
        if not line:
            totals.append([lax.psum(keep[index], "inp")[mask] for mask in range(n_tgt)])
            mine.append(to_owners(totals[-1], n_tgt))
            other.append(to_owners([lax.psum(send[index], "inp")[mask] for mask in range(n_tgt)], n_tgt))
        else:
            value = pair_sums[index]
            earlier = [part for total in totals[-1:] for part in total]
            arrived = lax.ppermute(after(value, *earlier), "inp", [(0, 3), (3, 0), (1, 2), (2, 1)])
            totals.append(plus(after(value, *others), arrived, spread=True))
            mine.append(to_owners(totals[-1], n_tgt))
            other.append(lax.ppermute(mine[-1], "inp", partners(n_inp, 1)))
        return totals[-1]

    for layer in range(layers):
        ready = flat if layer else [keys[1], along[1][0]]
        own_stats = row_stats(after(places[layer], *ready), keys[layer], values[layer], pieces[layer])
        stats.append(everywhere(own_stats, n_inp))
        results = attention_grads(
            after(places[layer], *flat), keys[layer], values[layer], pieces[layer], stats[layer]
        )
        keep += results[:PARTS]
        send += results[PARTS : 2 * PARTS]
        flat += results[2 * PARTS :]
    send[0] = after(send[0], *stats[-1])
    chunks = len(keep)

    sent = back_blocks(orders[0], wk, wv, flat, share, BF16)
    pair_sum(sent)
    while len(pair_sums) < chunks:
        send[len(pair_sums)] = after(send[len(pair_sums)], pair_sums[-1])
        pair_sum()
    arrived = lax.ppermute(after(sent, pair_sums[0]), "tgt", partners(n_tgt, 1))
    own_blocks = back_blocks(after(orders[1], pair_sums[0]), wk, wv, flat, share, F32)
    arrived = after(arrived, pair_sums[0])
    far_own, far_other = (total_of([(own_blocks, side), (arrived, side)]) for side in range(2))
    waits = [far_own, far_other]
    far_other = lax.ppermute(far_other, "tgt", partners(n_tgt, 2))
    far_own = lax.ppermute(far_own, "tgt", partners(n_tgt, 2))
    line_sum(*waits)
    side_own = total_of([(own_blocks, 3), (arrived, 3), (after(far_other, mine[0]), 0)])
    side_own = lax.ppermute(side_own, "mdl", partners(n_mdl, 1))
    while len(totals) < chunks:
        line_sum(far_own, mine[0])
    query_grads = None
    for layer in range(layers):
        query_grads = join_heads(place, mine[layer], True, layer, layers, query_grads)
        query_grads = join_heads(place, other[layer], False, layer, layers, query_grads)
    enc_grad = total_of([(own_blocks, 2), (arrived, 2), (far_own, 0), (side_own, 0)])
    return query_grads, enc_grad[0]


def solution(mesh):
    placed = (
        P("inp", None),
        P(None, None, "mdl", "tgt", None),
        P(None, None, "mdl", "tgt", None),
        P(None, "tgt", "mdl", None),
        P(None, "tgt", "mdl", None),
    )
    return jax.shard_map(
        body,
        mesh=mesh,
        in_specs=placed,
        out_specs=(P(None, "tgt", "mdl", None), P("inp", ("tgt", "mdl"))),
        check_vma=False,
    )
```
